128 devices in a mesh: strip: 128 (over z, x, y, core).
Axes of the slice: x: 4, y: 4, z: 4, core: 2. Of those that a mesh axis runs over, the one named last changes fastest.
Arguments:
- features: bfloat16 [128, 1920, 384], P(None, 'strip'), may hold values from -6 to 6
- grad_out: bfloat16 [128, 1920, 384], P(None, 'strip'), may hold values from -6 to 6
- widths: int32 [128], replicated, may hold values from 3 to 15, as said below
- dw_kernel: bfloat16 [49, 384], replicated, may hold values from -0.875 to 0.875
- dw_bias: bfloat16 [384], replicated, may hold values from -3 to 3
- ln_gain: bfloat16 [384], replicated, may hold values from 0.25 to 1.75
- ln_bias: bfloat16 [384], replicated, may hold values from -3 to 3
- w_in: bfloat16 [384, 1536], P(None, 'strip'), may hold values from -0.3125 to 0.3125
- in_bias: bfloat16 [1536], P('strip'), may hold values from -3 to 3
- w_out: bfloat16 [1536, 384], P('strip'), may hold values from -0.15625 to 0.15625
- out_bias: bfloat16 [384], replicated, may hold values from -3 to 3
- layer_scale: bfloat16 [384], replicated, may hold values from 0.5 to 2
Outputs:
- d_input: bfloat16 [128, 1920, 384], P(None, 'strip')
- g_dw_kernel: float32 [49, 384], replicated
- g_dw_bias: float32 [384], replicated
- g_ln_gain: float32 [384], replicated
- g_ln_bias: float32 [384], replicated
- g_w_in: float32 [384, 1536], P(None, 'strip')
- g_in_bias: float32 [1536], P('strip')
- g_w_out: float32 [1536, 384], P('strip')
- g_out_bias: float32 [384], replicated
- g_layer_scale: float32 [384], replicated
The draws below stay inside these ranges and needn't reach their ends.
Inputs may be any that keep to these rules, and one draw needn't show every extreme that they name: Device d's strip fills its first widths[d] slots; strips lie side by side in device order and cover all 640 columns. Every aligned group of 8 devices (devices 8k to 8k+7) holds exactly 40 columns in all. Exactly one strip has 15 columns; every other strip is narrower.
All inputs are finite; a program needn't handle non-finite values.
Results may differ from the reference program's by a relative error of at most 0.009.
Values may be sent and summed in bfloat16 or wider, within the bound.
A program may use at most 128 MiB of HBM per device.

```python
import math
import jax
import jax.numpy as jnp
from jax import lax

C = 384
FF = 1536
ROWS = 128
COL_DEV = 5
CAP = 15
COLS = 640
TOKENS = 81920
N_STRIP = 128


def draw_widths(key, part):
    device_count = COLS // COL_DEV
    mean_cols = COL_DEV
    group_count = device_count // 8
    key_pairs, key_roll, key_place, key_order = jax.random.split(key, 4)
    offsets = jax.random.randint(key_pairs, (device_count // 2,), -(mean_cols - 3), mean_cols - 2)
    paired = jnp.stack([mean_cols + offsets, mean_cols - offsets], axis=1).reshape(device_count).astype(jnp.int32)
    base_share = 5 * mean_cols // 7
    extra_count = 5 * mean_cols - 7 * base_share
    others = (base_share + (jnp.arange(7) < extra_count).astype(jnp.int32)).astype(jnp.int32)
    heavy_group = jnp.concatenate([jnp.full((1,), 3 * mean_cols, jnp.int32), others])
    heavy_group = jnp.roll(heavy_group, jax.random.randint(key_roll, (), 0, 8))
    place_at = (jax.random.randint(key_place, (), 0, group_count) * 8).astype(jnp.int32)
    placed = lax.dynamic_update_slice(paired, heavy_group, (place_at,)).astype(jnp.int32)
    group_keys = jax.random.split(key_order, group_count)
    orders = jax.vmap(lambda group_key: jax.random.permutation(group_key, 8))(group_keys).astype(jnp.int32)
    shuffled = jnp.take_along_axis(placed.reshape(group_count, 8), orders, axis=1)
    return shuffled.reshape(device_count).astype(jnp.int32)


def block_levels(stream_key, dims, shards, low, largest):
    gain, own = 1.0, jax.random.fold_in(stream_key, 6)
    for position, shards_of in shards:
        draws = jnp.exp(jax.random.uniform(jax.random.fold_in(own, position), (shards_of,), jnp.float32, low / len(shards), largest / len(shards)))
        gain = gain * jnp.repeat(draws, dims[position] // shards_of).reshape([-1 if axis == position else 1 for axis in range(len(dims))])
    return gain


def scatter_about(stream_key, extent, width, most, pieces=(), kind=jnp.bfloat16):
    result = width * jax.random.normal(stream_key, extent, jnp.float32)
    if pieces:
        result = result * block_levels(stream_key, extent, pieces, -0.22, 0.18)
    return jnp.clip(result, -most, most).astype(kind)


def setup_inputs(seed: int = 0) -> dict:
    key_of = jax.random.split(jax.random.key(seed), 13)
    return {
        "features": scatter_about(key_of[0], (ROWS, N_STRIP * CAP, C), 1.0, 6.0, ((1, 128),)),
        "grad_out": scatter_about(key_of[1], (ROWS, N_STRIP * CAP, C), 1.0, 6.0, ((1, 128),)),
        "widths": draw_widths(jax.random.fold_in(key_of[12], 71), 0),
        "dw_kernel": scatter_about(key_of[3], (49, C), 49 ** -0.5, 0.875),
        "dw_bias": scatter_about(key_of[4], (C,), 0.5, 3.0),
        "ln_gain": jnp.clip(1.0 + 0.15 * jax.random.normal(key_of[5], (C,), jnp.float32), 0.25, 1.75).astype(jnp.bfloat16),
        "ln_bias": scatter_about(key_of[6], (C,), 0.5, 3.0),
        "w_in": scatter_about(key_of[7], (C, FF), C ** -0.5, 0.3125, ((1, 128),)),
        "in_bias": scatter_about(key_of[8], (FF,), 0.5, 3.0, ((0, 128),)),
        "w_out": scatter_about(key_of[9], (FF, C), FF ** -0.5, 0.15625, ((0, 128),)),
        "out_bias": scatter_about(key_of[10], (C,), 0.5, 3.0),
        "layer_scale": jnp.clip(jnp.exp(jax.random.uniform(key_of[11], (C,), jnp.float32, math.log(0.5), math.log(2.0))), 0.5, 2.0).astype(jnp.bfloat16),
    }


inv_root_two = 0.7071067811865476
inv_root_tau = 0.3989422804014327
ln_eps = 1e-06

def slot_table(widths):
    starts = (jnp.cumsum(widths) - widths).astype(jnp.int32)
    columns = jnp.arange(COLS, dtype=jnp.int32)
    owners = (lax.optimization_barrier(jnp.sum((starts[None, :] <= columns[:, None]).astype(jnp.int32), axis=1)) - 1).astype(jnp.int32)
    return (owners * CAP + columns - starts[owners]).astype(jnp.int32)

def conv_taps(padded, kernel, row_count, col_count):
    summed = jnp.zeros((row_count, col_count, padded.shape[2]), jnp.float32)
    for tap_row in range(7):
        for tap_col in range(7):
            summed = summed + kernel[tap_row * 7 + tap_col] * padded[tap_row:tap_row + row_count, tap_col:tap_col + col_count]
    return summed

def kernel_terms(d_conv32, padded, row_count, col_count):
    return jnp.stack([lax.optimization_barrier(jnp.sum(d_conv32 * padded[tap_row:tap_row + row_count, tap_col:tap_col + col_count], axis=(0, 1))) for tap_row in range(7) for tap_col in range(7)])

def flipped(kernel):
    return kernel.reshape(7, 7, -1)[::-1, ::-1].reshape(49, -1)

def mlp_back(conv_out, cotangent, w_in, in_bias, w_out, out_bias, ln_gain, ln_bias, layer_scale):
    values = conv_out.astype(jnp.float32)
    mean_val = lax.optimization_barrier(jnp.mean(values, axis=-1, keepdims=True))
    centred = values - mean_val
    inv_std = lax.rsqrt(lax.optimization_barrier(jnp.mean(centred * centred, axis=-1, keepdims=True)) + ln_eps)
    normed_raw = centred * inv_std
    normed = (normed_raw * ln_gain.astype(jnp.float32) + ln_bias.astype(jnp.float32)).astype(jnp.bfloat16)
    pre_act = jnp.dot(normed, w_in, preferred_element_type=jnp.float32) + in_bias.astype(jnp.float32)
    cdf_part = 0.5 * (1.0 + lax.erf(pre_act * inv_root_two))
    activated = (pre_act * cdf_part).astype(jnp.bfloat16)
    mlp_out = jnp.dot(activated, w_out, preferred_element_type=jnp.float32) + out_bias.astype(jnp.float32)
    cot_wide = cotangent.astype(jnp.float32)
    g_scale = lax.optimization_barrier(jnp.sum(cot_wide * mlp_out, axis=0))
    d_mlp = (cot_wide * layer_scale.astype(jnp.float32)).astype(jnp.bfloat16)
    g_obias = lax.optimization_barrier(jnp.sum(d_mlp.astype(jnp.float32), axis=0))
    g_wout = lax.dot_general(activated, d_mlp, (((0,), (0,)), ((), ())), preferred_element_type=jnp.float32)
    d_act = lax.dot_general(d_mlp, w_out, (((1,), (1,)), ((), ())), preferred_element_type=jnp.float32)
    slope = cdf_part + pre_act * jnp.exp(-0.5 * pre_act * pre_act) * inv_root_tau
    d_pre = (d_act * slope).astype(jnp.bfloat16)
    g_ibias = lax.optimization_barrier(jnp.sum(d_pre.astype(jnp.float32), axis=0))
    g_win = lax.dot_general(normed, d_pre, (((0,), (0,)), ((), ())), preferred_element_type=jnp.float32)
    d_norm = lax.dot_general(d_pre, w_in, (((1,), (1,)), ((), ())), preferred_element_type=jnp.float32)
    g_lgain = lax.optimization_barrier(jnp.sum(d_norm * normed_raw, axis=0))
    g_lbias = lax.optimization_barrier(jnp.sum(d_norm, axis=0))
    scaled = d_norm * ln_gain.astype(jnp.float32)
    d_conv = (inv_std * (scaled - lax.optimization_barrier(jnp.mean(scaled, axis=-1, keepdims=True)) - normed_raw * lax.optimization_barrier(jnp.mean(scaled * normed_raw, axis=-1, keepdims=True)))).astype(jnp.bfloat16)
    return (d_conv, (g_win, g_ibias, g_wout, g_obias, g_lgain, g_lbias, g_scale))

def reference(features, grad_out, widths, dw_kernel, dw_bias, ln_gain, ln_bias, w_in, in_bias, w_out, out_bias, layer_scale):
    slot_ids = slot_table(widths)
    window_feat = features[:, slot_ids, :]
    cotangent = grad_out[:, slot_ids, :]
    kernel = dw_kernel.astype(jnp.float32)
    padded = jnp.pad(window_feat.astype(jnp.float32), ((3, 3), (3, 3), (0, 0)))
    conv_out = (conv_taps(padded, kernel, ROWS, COLS) + dw_bias.astype(jnp.float32)).astype(jnp.bfloat16)
    blocks = ROWS // 8

    def block_step(carried, block_pair):
        d_conv, grads = mlp_back(block_pair[0], block_pair[1], w_in, in_bias, w_out, out_bias, ln_gain, ln_bias, layer_scale)
        return (tuple((left_part + right_part for left_part, right_part in zip(carried, grads))), d_conv)
    starting = (jnp.zeros((C, FF), jnp.float32), jnp.zeros((FF,), jnp.float32), jnp.zeros((FF, C), jnp.float32), jnp.zeros((C,), jnp.float32), jnp.zeros((C,), jnp.float32), jnp.zeros((C,), jnp.float32), jnp.zeros((C,), jnp.float32))
    totals, d_blocks = lax.scan(block_step, starting, (conv_out.reshape(blocks, 8 * COLS, C), cotangent.reshape(blocks, 8 * COLS, C)))
    d_conv32 = d_blocks.reshape(ROWS, COLS, C).astype(jnp.float32)
    g_kernel = kernel_terms(d_conv32, padded, ROWS, COLS)
    g_dwbias = lax.optimization_barrier(jnp.sum(d_conv32, axis=(0, 1)))
    d_padded = jnp.pad(d_conv32, ((3, 3), (3, 3), (0, 0)))
    d_image = (cotangent.astype(jnp.float32) + conv_taps(d_padded, flipped(kernel), ROWS, COLS)).astype(jnp.bfloat16)
    d_input = jnp.zeros((ROWS, N_STRIP * CAP, C), jnp.bfloat16).at[:, slot_ids, :].set(d_image)
    grad_scale = 1.0 / math.sqrt(TOKENS)
    g_win, g_ibias, g_wout, g_obias, g_lgain, g_lbias, g_scale = totals
    return (d_input, g_kernel * grad_scale, g_dwbias * grad_scale, g_lgain * grad_scale, g_lbias * grad_scale, g_win * grad_scale, g_ibias * grad_scale, g_wout * grad_scale, g_obias * grad_scale, g_scale * grad_scale)
```

```python
import functools, math
import jax, jax.numpy as jnp
from jax import lax
from jax.sharding import PartitionSpec as P
from jax.experimental import pallas as pl
from jax.experimental.pallas import tpu as pltpu

ROWS, C, FF, CAP = 128, 384, 1536, 15
NCOL = 16
XCOL = NCOL + 6
RP = ROWS + 16
F32, BF16 = jnp.float32, jnp.bfloat16
VMEM = pl.BlockSpec(memory_space=pltpu.VMEM)
SMEM = pl.BlockSpec(memory_space=pltpu.SMEM)


def gelu_parts(x):
    e = jnp.exp(x * x * -0.5)
    t = 1.0 / (1.0 + (0.3275911 * 0.7071067811865476) * jnp.abs(x))
    q = ((((0.5 * 1.061405429) * t - 0.5 * 1.453152027) * t + 0.5 * 1.421413741) * t - 0.5 * 0.284496736) * t + 0.5 * 0.254829592
    h = q * t * e
    cdf = jnp.where(x >= 0, 1.0 - h, h)
    slope = cdf + x * e * 0.3989422804014327
    return x * cdf, slope


def fill_taps(taps_ref, tapb, flip):
    def body(i, _):
        src = 48 - i if flip else i
        row = taps_ref[pl.ds(src, 1), :]
        for g in range(3):
            tapb[i, g] = jnp.broadcast_to(row[:, g * 128:(g + 1) * 128], (8, 128))
        return 0
    lax.fori_loop(0, 49, body, 0)


def fill_ext(xf, own, from_left, from_right, n, has_left, has_right):
    zero = jnp.zeros((8, 128), F32)
    def edge(i, _):
        for g in range(3):
            xf[i, g, 0:8, :] = zero
            xf[i, g, RP - 8:RP, :] = zero
        return 0
    lax.fori_loop(0, XCOL, edge, 0)
    def put(dst, block):
        block = block.astype(F32)
        for g in range(3):
            xf[dst, g, 8:8 + ROWS, :] = block[:, g * 128:(g + 1) * 128]
    def blank(i, _):
        put(i, jnp.zeros((ROWS, C), BF16))
        return 0
    lax.fori_loop(n + 6, XCOL, blank, 0)
    def col(i, _):
        put(i + 3, own[i])
        return 0
    lax.fori_loop(0, n, col, 0)
    for i in range(3):
        put(i, jnp.where(has_left, from_left[i].astype(F32), 0.0))
        put(n + 3 + i, jnp.where(has_right, from_right[i].astype(F32), 0.0))


def conv_cols(xf, tapb, g, j0, r0, J):
    accs = [None] * J
    for a in range(7):
        xs = [xf[j0 + i, g, pl.ds(r0 + 5 + a, 8), :] for i in range(J + 6)]
        for b in range(7):
            t = tapb[a * 7 + b, g]
            for j in range(J):
                p = t * xs[j + b]
                accs[j] = p if accs[j] is None else accs[j] + p
    return accs


def k2_kernel(n_ref, feat, fl, fr, cot, taps, vecs, w1t_ref, w2t_ref,
              dconv, edge_l, edge_r, g1_out, g2_out, vec_out,
              xf, tapb, conv, w1, w2, g1, g2, vacc):
    n, has_left, has_right = n_ref[0], n_ref[1] > 0, n_ref[2] > 0
    fill_taps(taps, tapb, False)
    fill_ext(xf, feat, fl, fr, n, has_left, has_right)
    for f in range(FF // 256):
        sl = pl.ds(f * 256, 256)
        w1[:, sl] = w1t_ref[sl, :].T
        w2[:, sl] = w2t_ref[sl, :].T
    J = 4
    def jloop(jb, _):
        def gloop(g, _):
            bias = vecs[0:1, :]
            def rloop(r, _):
                r0 = r * 8
                accs = conv_cols(xf, tapb, g, jb * J, r0, J)
                for j in range(J):
                    conv[jb * J + j, g, pl.ds(pl.multiple_of(r0, 8), 8), :] = accs[j]
                return 0
            lax.fori_loop(0, 16, rloop, 0)
            return 0
        lax.fori_loop(0, 3, gloop, 0)
        return 0
    lax.fori_loop(0, (n + J - 1) // J, jloop, 0)

    bias, gain, lbias, ls = vecs[0:1, :], vecs[1:2, :], vecs[2:3, :], vecs[3:4, :]
    def zero_col(i, _):
        dconv[i] = jnp.zeros((ROWS, C), BF16)
        return 0
    lax.fori_loop(0, NCOL, zero_col, 0)
    vacc[...] = jnp.zeros_like(vacc)
    g1[...] = jnp.zeros_like(g1)
    g2[...] = jnp.zeros_like(g2)
    T = 2 * ROWS
    one_col = (lax.broadcasted_iota(jnp.int32, (T, 128), 1) == 0).astype(BF16)

    def part(x):
        return x.reshape(T // 8, 8, C).sum(0)

    def step(s, _):
        v = jnp.concatenate([conv[pl.ds(2 * s, 2), g].reshape(T, 128) for g in range(3)], axis=1) + bias
        v = v.astype(BF16).astype(F32)
        mean = jnp.sum(v, axis=1, keepdims=True) * (1.0 / C)
        cen = v - mean
        inv = lax.rsqrt(jnp.sum(cen * cen, axis=1, keepdims=True) * (1.0 / C) + 1e-6)
        nraw = cen * inv
        normed = jnp.concatenate([(nraw * gain + lbias).astype(BF16), one_col], axis=1)
        dm32 = cot[pl.ds(2 * s, 2)].reshape(T, C).astype(F32) * ls
        dmlp = dm32.astype(BF16)
        vacc[2] += part(dmlp.astype(F32))
        normed_t = normed.T
        dmlp_t = dmlp.T
        dn = jnp.zeros((T, C), F32)
        for f in range(FF // 256):
            sl = slice(f * 256, f * 256 + 256)
            pre = jnp.dot(normed, w1[:, sl], preferred_element_type=F32)
            dact = jnp.dot(dmlp, w2[:, sl], preferred_element_type=F32)
            act, slope = gelu_parts(pre)
            act = act.astype(BF16)
            dpre = (dact * slope).astype(BF16)
            g1[:, sl] += jnp.dot(normed_t, dpre, preferred_element_type=F32)
            g2[:, sl] += jnp.dot(dmlp_t, act, preferred_element_type=F32)
            dn += jnp.dot(dpre, w1t_ref[sl, 0:C], preferred_element_type=F32)
        vacc[0] += part(dn * nraw)
        vacc[1] += part(dn)
        sc = dn * gain
        m1 = jnp.sum(sc, axis=1, keepdims=True) * (1.0 / C)
        m2 = jnp.sum(sc * nraw, axis=1, keepdims=True) * (1.0 / C)
        dc = (inv * (sc - m1 - nraw * m2)).astype(BF16)
        vacc[4] += part(dc.astype(F32))
        dconv[pl.ds(2 * s, 2)] = dc.reshape(2, ROWS, C)
        return 0
    lax.fori_loop(0, (n + 1) // 2, step, 0)

    for i in range(3):
        edge_l[i] = dconv[i]
        edge_r[i] = dconv[n - 3 + i]
    srow = jnp.zeros((8, C), F32)
    for f in range(FF // 128):
        sl = slice(f * 128, f * 128 + 128)
        g1_out[sl, :] = g1[:, sl].T.astype(BF16)
        g2t = g2[:, sl].T
        g2_out[sl, :] = g2t.astype(BF16)
        srow += (g2t * w2t_ref[sl, :].astype(F32)).reshape(16, 8, C).sum(0)
    vacc[3] = srow
    rows = [jnp.sum(vacc[i], axis=0, keepdims=True) for i in range(5)]
    vec_out[...] = jnp.concatenate(rows + [jnp.zeros((3, C), F32)], axis=0)


def k2(n, feat, fl, fr, cot, taps, vecs, w1t, w2t):
    return pl.pallas_call(
        k2_kernel,
        out_shape=(
            jax.ShapeDtypeStruct((NCOL, ROWS, C), BF16),
            jax.ShapeDtypeStruct((3, ROWS, C), BF16),
            jax.ShapeDtypeStruct((3, ROWS, C), BF16),
            jax.ShapeDtypeStruct((FF, 512), BF16),
            jax.ShapeDtypeStruct((FF, C), BF16),
            jax.ShapeDtypeStruct((8, C), F32),
        ),
        in_specs=[SMEM] + [VMEM] * 8,
        out_specs=[VMEM] * 6,
        scratch_shapes=[
            pltpu.VMEM((XCOL, 3, RP, 128), F32),
            pltpu.VMEM((49, 3, 8, 128), F32),
            pltpu.VMEM((NCOL, 3, ROWS, 128), F32),
            pltpu.VMEM((512, FF), BF16),
            pltpu.VMEM((C, FF), BF16),
            pltpu.VMEM((512, FF), F32),
            pltpu.VMEM((C, FF), F32),
            pltpu.VMEM((8, 8, C), F32),
        ],
        compiler_params=pltpu.CompilerParams(vmem_limit_bytes=56 * 2**20),
        name="mlp_pass",
    )(n, feat, fl, fr, cot, taps, vecs, w1t, w2t)


def kernel_grads(xf, df, kacc, nb, J):
    def gloop(g, _):
        def aloop(a, _):
            def jloop(jb, accs):
                def rloop(r, accs):
                    r0 = r * 8
                    accs = list(accs)
                    ds = [df[jb * J + 3 + j, g, pl.ds(pl.multiple_of(r0 + 8, 8), 8), :] for j in range(J)]
                    xs = [xf[jb * J + i, g, pl.ds(r0 + 5 + a, 8), :] for i in range(J + 6)]
                    for b in range(7):
                        p = ds[0] * xs[b]
                        for j in range(1, J):
                            p = p + ds[j] * xs[j + b]
                        accs[b] = accs[b] + p
                    return tuple(accs)
                return lax.fori_loop(0, 16, rloop, accs, unroll=4)
            accs = lax.fori_loop(0, nb, jloop, tuple(jnp.zeros((8, 128), F32) for _ in range(7)))
            for b in range(7):
                kacc[a * 7 + b, g] = accs[b]
            return 0
        lax.fori_loop(0, 7, aloop, 0)
        return 0
    lax.fori_loop(0, 3, gloop, 0)


def k4_kernel(n_ref, feat, fl, fr, dconv, dl, dr, cot, taps, dimg, kg_out, xf, df, tapb, kacc):
    n, has_left, has_right = n_ref[0], n_ref[1] > 0, n_ref[2] > 0
    fill_taps(taps, tapb, True)
    fill_ext(xf, feat, fl, fr, n, has_left, has_right)
    zeros3 = jnp.zeros((3, ROWS, C), BF16)
    fill_ext(df, dconv, dl, zeros3, n, has_left, has_right)
    J = 4
    nb = (n + J - 1) // J
    kernel_grads(xf, df, kacc, nb, J)
    def kout(i, _):
        row = jnp.concatenate([jnp.sum(kacc[i, g], axis=0, keepdims=True) for g in range(3)], axis=1)
        kg_out[pl.ds(i, 1), :] = row
        return 0
    lax.fori_loop(0, 49, kout, 0)
    for i in range(3):
        block = jnp.where(has_right, dr[i].astype(F32), 0.0)
        for g in range(3):
            df[n + 3 + i, g, 8:8 + ROWS, :] = block[:, g * 128:(g + 1) * 128]

    def cjloop(jb, _):
        for g in range(3):
            ls = slice(g * 128, g * 128 + 128)
            def rloop(r, _):
                r0 = pl.multiple_of(r * 16, 16)
                lo = conv_cols(df, tapb, g, jb * J, r0, J)
                hi = conv_cols(df, tapb, g, jb * J, r0 + 8, J)
                for j in range(J):
                    col = jb * J + j
                    acc = jnp.concatenate([lo[j], hi[j]], axis=0) + cot[col, pl.ds(r0, 16), ls].astype(F32)
                    dimg[col, pl.ds(r0, 16), ls] = acc.astype(BF16)
                return 0
            lax.fori_loop(0, 8, rloop, 0)
        return 0
    lax.fori_loop(0, nb, cjloop, 0)
    def zero_col(i, _):
        dimg[i] = jnp.zeros((ROWS, C), BF16)
        return 0
    lax.fori_loop(n, NCOL, zero_col, 0)


def k4(n, feat, fl, fr, dconv, dl, dr, cot, taps):
    return pl.pallas_call(
        k4_kernel,
        out_shape=(
            jax.ShapeDtypeStruct((NCOL, ROWS, C), BF16),
            jax.ShapeDtypeStruct((56, C), F32),
        ),
        in_specs=[SMEM] + [VMEM] * 8,
        out_specs=[VMEM] * 2,
        scratch_shapes=[
            pltpu.VMEM((XCOL, 3, RP, 128), F32),
            pltpu.VMEM((XCOL, 3, RP, 128), F32),
            pltpu.VMEM((49, 3, 8, 128), F32),
            pltpu.VMEM((49, 3, 8, 128), F32),
        ],
        compiler_params=pltpu.CompilerParams(vmem_limit_bytes=56 * 2**20),
        name="conv_back",
    )(n, feat, fl, fr, dconv, dl, dr, cot, taps)


MESH = pl.DeviceIdType.MESH
N_DEV = 128


def place():
    me = lax.axis_index("strip")
    core = lax.rem(me, 2)
    y = lax.rem(me // 2, 4)
    x = lax.rem(me // 8, 4)
    z = me // 32
    return me, core, y, x, z


def peers_of(me, coord, stride):
    return [me + (lax.rem(coord + o, 4) - coord) * stride for o in (1, 2, 3)]


def greet(devices):
    barrier = pltpu.get_barrier_semaphore()
    for dev in devices:
        pl.semaphore_signal(barrier, inc=1, device_id=(dev,), device_id_type=MESH)
    pl.semaphore_wait(barrier, len(devices))


def send(src, dst, sems, idx, dev):
    copy = pltpu.make_async_remote_copy(
        src_ref=src, dst_ref=dst, send_sem=sems[0].at[idx], recv_sem=sems[1].at[idx],
        device_id=(dev,), device_id_type=MESH)
    copy.start()
    return copy


def wait_all(copies):
    for copy in copies:
        copy.wait()


def k1_kernel(s1, s2, el, er, w1_out, w2_out, fl_out, fr_out,
              bx1, bx2, w1, w2, fl, fr, ssem, rsem):
    me, core, y, x, z = place()
    xs, ys, zs = peers_of(me, x, 8), peers_of(me, y, 2), peers_of(me, z, 32)
    mate = me + 1 - 2 * core
    right, left = lax.rem(me + 1, N_DEV), lax.rem(me + N_DEV - 1, N_DEV)
    sems = (ssem, rsem)
    greet(xs + ys + zs + [mate, left, right])
    first = []
    for o in range(3):
        first.append(send(s1, bx1.at[x], sems, o, xs[o]))
        first.append(send(s2, bx2.at[x], sems, 3 + o, xs[o]))
    halo = [send(er, fl, sems, 6, right), send(el, fr, sems, 7, left)]
    bx1[x] = s1[...]
    bx2[x] = s2[...]
    wait_all(first)
    w1[core, z, y] = jnp.concatenate([bx1[q].astype(F32)[:12] for q in range(4)], axis=0).astype(BF16)
    w2[core, z, y] = jnp.concatenate([bx2[q].astype(F32)[:12] for q in range(4)], axis=0).astype(BF16)
    second = []
    for o in range(3):
        second.append(send(w1.at[core, z, y], w1.at[core, z, y], sems, 8 + o, ys[o]))
        second.append(send(w2.at[core, z, y], w2.at[core, z, y], sems, 11 + o, zs[o]))
    wait_all(second)
    third = []
    for o in range(3):
        third.append(send(w1.at[core, z], w1.at[core, z], sems, 14 + o, zs[o]))
        third.append(send(w2.at[core, :, y], w2.at[core, :, y], sems, 17 + o, ys[o]))
    wait_all(third)
    fourth = [send(w1.at[core], w1.at[core], sems, 20, mate), send(w2.at[core], w2.at[core], sems, 21, mate)]
    wait_all(halo)
    fl_out[...] = fl[...]
    fr_out[...] = fr[...]
    wait_all(fourth)
    w1_out[...] = w1[...]
    w2_out[...] = w2[...]


def k1(s1, s2, el, er):
    return pl.pallas_call(
        k1_kernel,
        out_shape=(
            jax.ShapeDtypeStruct((2, 4, 4, 48, 512), BF16),
            jax.ShapeDtypeStruct((2, 4, 4, 48, C), BF16),
            jax.ShapeDtypeStruct((3, ROWS, C), BF16),
            jax.ShapeDtypeStruct((3, ROWS, C), BF16),
        ),
        in_specs=[VMEM] * 4,
        out_specs=[VMEM] * 4,
        scratch_shapes=[
            pltpu.VMEM((4, 16, 512), BF16),
            pltpu.VMEM((4, 16, C), BF16),
            pltpu.VMEM((2, 4, 4, 48, 512), BF16),
            pltpu.VMEM((2, 4, 4, 48, C), BF16),
            pltpu.VMEM((3, ROWS, C), BF16),
            pltpu.VMEM((3, ROWS, C), BF16),
            pltpu.SemaphoreType.DMA((22,)),
            pltpu.SemaphoreType.DMA((22,)),
        ],
        compiler_params=pltpu.CompilerParams(collective_id=0, has_side_effects=True, vmem_limit_bytes=40 * 2**20),
        name="gather_weights",
    )(s1, s2, el, er)


def k3_kernel(g1, g2, el, er, o1, o2, fl_out, fr_out,
              rc1, rc2, c1, c2, rz1, ry2, t1, t2, ry1, rz2, p1, p2, rx1, rx2, fl, fr, ssem, rsem):
    me, core, y, x, z = place()
    xs, ys, zs = peers_of(me, x, 8), peers_of(me, y, 2), peers_of(me, z, 32)
    mate = me + 1 - 2 * core
    right, left = lax.rem(me + 1, N_DEV), lax.rem(me + N_DEV - 1, N_DEV)
    sems = (ssem, rsem)
    greet(xs + ys + zs + [mate, left, right])
    first = [send(g1.at[1 - core], rc1, sems, 0, mate), send(g2.at[1 - core], rc2, sems, 1, mate)]
    halo = [send(er, fl, sems, 2, right), send(el, fr, sems, 3, left)]
    wait_all(first)

    def add_first(i, _):
        zi, yi = i // 4, lax.rem(i, 4)
        c1[zi, yi] = (g1[core, zi, yi].astype(F32) + rc1[zi, yi].astype(F32)).astype(BF16)
        c2[zi, yi] = (g2[core, zi, yi].astype(F32) + rc2[zi, yi].astype(F32)).astype(BF16)
        return 0
    lax.fori_loop(0, 16, add_first, 0)
    second = []
    for o in range(3):
        second.append(send(c1.at[lax.rem(z + o + 1, 4)], rz1.at[o], sems, 4 + o, zs[o]))
        second.append(send(c2.at[:, lax.rem(y + o + 1, 4)], ry2.at[o], sems, 7 + o, ys[o]))
    wait_all(second)

    def add_second(i, _):
        t1[i] = (c1[z, i].astype(F32) + rz1[0, i].astype(F32) + rz1[1, i].astype(F32) + rz1[2, i].astype(F32)).astype(BF16)
        t2[i] = (c2[i, y].astype(F32) + ry2[0, i].astype(F32) + ry2[1, i].astype(F32) + ry2[2, i].astype(F32)).astype(BF16)
        return 0
    lax.fori_loop(0, 4, add_second, 0)
    third = []
    for o in range(3):
        third.append(send(t1.at[lax.rem(y + o + 1, 4)], ry1.at[o], sems, 10 + o, ys[o]))
        third.append(send(t2.at[lax.rem(z + o + 1, 4)], rz2.at[o], sems, 13 + o, zs[o]))
    wait_all(third)
    u1 = t1[y].astype(F32) + ry1[0].astype(F32) + ry1[1].astype(F32) + ry1[2].astype(F32)
    u2 = t2[z].astype(F32) + rz2[0].astype(F32) + rz2[1].astype(F32) + rz2[2].astype(F32)
    for q in range(4):
        p1[q, 0:12, :] = u1[q * 12:q * 12 + 12]
        p2[q, 0:12, :] = u2[q * 12:q * 12 + 12]
        p1[q, 12:16, :] = jnp.zeros((4, 512), F32)
        p2[q, 12:16, :] = jnp.zeros((4, C), F32)
    fourth = []
    for o in range(3):
        q = lax.rem(x + o + 1, 4)
        fourth.append(send(p1.at[q], rx1.at[o], sems, 16 + o, xs[o]))
        fourth.append(send(p2.at[q], rx2.at[o], sems, 19 + o, xs[o]))
    wait_all(halo)
    fl_out[...] = fl[...]
    fr_out[...] = fr[...]
    wait_all(fourth)
    o1[...] = p1[x] + rx1[0] + rx1[1] + rx1[2]
    o2[...] = p2[x] + rx2[0] + rx2[1] + rx2[2]


def k3(g1, g2, el, er):
    return pl.pallas_call(
        k3_kernel,
        out_shape=(
            jax.ShapeDtypeStruct((16, 512), F32),
            jax.ShapeDtypeStruct((16, C), F32),
            jax.ShapeDtypeStruct((3, ROWS, C), BF16),
            jax.ShapeDtypeStruct((3, ROWS, C), BF16),
        ),
        in_specs=[VMEM] * 4,
        out_specs=[VMEM] * 4,
        scratch_shapes=[
            pltpu.VMEM((4, 4, 48, 512), BF16),
            pltpu.VMEM((4, 4, 48, C), BF16),
            pltpu.VMEM((4, 4, 48, 512), BF16),
            pltpu.VMEM((4, 4, 48, C), BF16),
            pltpu.VMEM((3, 4, 48, 512), BF16),
            pltpu.VMEM((3, 4, 48, C), BF16),
            pltpu.VMEM((4, 48, 512), BF16),
            pltpu.VMEM((4, 48, C), BF16),
            pltpu.VMEM((3, 48, 512), BF16),
            pltpu.VMEM((3, 48, C), BF16),
            pltpu.VMEM((4, 16, 512), F32),
            pltpu.VMEM((4, 16, C), F32),
            pltpu.VMEM((3, 16, 512), F32),
            pltpu.VMEM((3, 16, C), F32),
            pltpu.VMEM((3, ROWS, C), BF16),
            pltpu.VMEM((3, ROWS, C), BF16),
            pltpu.SemaphoreType.DMA((22,)),
            pltpu.SemaphoreType.DMA((22,)),
        ],
        compiler_params=pltpu.CompilerParams(collective_id=1, has_side_effects=True, vmem_limit_bytes=40 * 2**20),
        name="scatter_grads",
    )(g1, g2, el, er)


def k5_kernel(kg, vec, out, cur, slots, ssem, rsem):
    me, core, y, x, z = place()
    xs, ys, zs = peers_of(me, x, 8), peers_of(me, y, 2), peers_of(me, z, 32)
    mate = me + 1 - 2 * core
    sems = (ssem, rsem)
    greet(xs + ys + zs + [mate])
    cur[0, 0:56, :] = kg[...]
    cur[0, 56:64, :] = vec[...]
    at = 0
    for stage, group in enumerate(([mate], ys, zs, xs)):
        copies = []
        for dev in group:
            copies.append(send(cur.at[stage], slots.at[at], sems, at, dev))
            at += 1
        wait_all(copies)
        total = cur[stage]
        for i in range(len(group)):
            total = total + slots[at - len(group) + i]
        if stage == 3:
            out[...] = total
        else:
            cur[stage + 1] = total


def k5(kg, vec):
    return pl.pallas_call(
        k5_kernel,
        out_shape=jax.ShapeDtypeStruct((64, C), F32),
        in_specs=[VMEM] * 2,
        out_specs=VMEM,
        scratch_shapes=[
            pltpu.VMEM((4, 64, C), F32),
            pltpu.VMEM((10, 64, C), F32),
            pltpu.SemaphoreType.DMA((10,)),
            pltpu.SemaphoreType.DMA((10,)),
        ],
        compiler_params=pltpu.CompilerParams(collective_id=2, has_side_effects=True),
        name="sum_vectors",
    )(kg, vec)


def local(features, grad_out, widths, dw_kernel, dw_bias, ln_gain, ln_bias,
          w_in, in_bias, w_out, out_bias, layer_scale):
    me = lax.axis_index("strip")
    n = lax.dynamic_index_in_dim(widths, me, keepdims=False)
    scal = jnp.stack([n, (me > 0).astype(jnp.int32), (me < N_DEV - 1).astype(jnp.int32)])
    mask = (jnp.arange(CAP, dtype=jnp.int32) < n)[:, None, None]

    def columns(a):
        a = jnp.where(mask, jnp.transpose(a, (1, 0, 2)), jnp.zeros((), a.dtype))
        return jnp.pad(a, ((0, NCOL - CAP), (0, 0), (0, 0)))
    feat, cot = columns(features), columns(grad_out)
    el = feat[:3]
    er = lax.dynamic_slice_in_dim(feat, n - 3, 3, 0)
    s1 = jnp.pad(jnp.concatenate([w_in.T, in_bias[:, None]], axis=1), ((0, 4), (0, 127)))
    s2 = jnp.pad(w_out, ((0, 4), (0, 0)))
    taps = dw_kernel.astype(F32)
    vecs = jnp.pad(jnp.stack([dw_bias, ln_gain, ln_bias, layer_scale]).astype(F32), ((0, 4), (0, 0)))
    w1t, w2t, fl, fr = k1(s1, s2, el, er)
    dconv, del_, der, g1, g2, vec = k2(scal, feat, fl, fr, cot, taps, vecs,
                                       w1t.reshape(FF, 512), w2t.reshape(FF, C))
    o1, o2, dl, dr = k3(g1.reshape(2, 4, 4, 48, 512), g2.reshape(2, 4, 4, 48, C), del_, der)
    dimg, kg = k4(scal, feat, fl, fr, dconv, dl, dr, cot, taps)
    total = k5(kg, vec)
    s = 1.0 / math.sqrt(ROWS * N_DEV * 5)
    ls, ob = layer_scale.astype(F32), out_bias.astype(F32)
    g_scale = (total[59] + ob * total[58]) / ls
    d_input = jnp.transpose(dimg[:CAP], (1, 0, 2))
    return (d_input, total[:49] * s, total[60] * s, total[56] * s, total[57] * s,
            o1[:12, :C].T * s, o1[:12, C] * s, o2[:12] * s, total[58] * s, g_scale * s)


def solution(mesh):
    wide = P(None, "strip", None)
    return jax.shard_map(
        local, mesh=mesh,
        in_specs=(wide, wide, P(), P(), P(), P(), P(), P(None, "strip"), P("strip"), P("strip", None), P(), P()),
        out_specs=(wide, P(), P(), P(), P(), P(None, "strip"), P("strip"), P("strip", None), P(), P()),
        check_vma=False)
```

```python
import math

import jax
import jax.numpy as jnp
from jax import lax
from jax.sharding import PartitionSpec as P
from jax.experimental import pallas as pl
from jax.experimental.pallas import tpu as pltpu

ROWS, C, FF, CAP = 128, 384, 1536, 15
N_DEV = 128
NC = 12
XC = NC + 6
RP = ROWS + 16
J = 4
T = 2 * ROWS
F32, BF16 = jnp.float32, jnp.bfloat16
VMEM = pl.BlockSpec(memory_space=pltpu.VMEM)
SMEM = pl.BlockSpec(memory_space=pltpu.SMEM)
MESH = pl.DeviceIdType.MESH
SCALE = 1.0 / math.sqrt(ROWS * N_DEV * 5)


def gelu_parts(x):
    e = jnp.exp(x * x * -0.5)
    t = 1.0 / (1.0 + (0.3275911 * 0.7071067811865476) * jnp.abs(x))
    q = ((((0.5 * 1.061405429) * t - 0.5 * 1.453152027) * t + 0.5 * 1.421413741) * t - 0.5 * 0.284496736) * t + 0.5 * 0.254829592
    h = q * t * e
    cdf = jnp.where(x >= 0, 1.0 - h, h)
    slope = cdf + x * e * 0.3989422804014327
    return x * cdf, slope


def fill_taps(taps_ref, tapb, flip):
    for g in range(3):
        block = taps_ref[:, g * 128:(g + 1) * 128].astype(F32)
        for i in range(49):
            src = 48 - i if flip else i
            tapb[i, g] = jnp.broadcast_to(block[src:src + 1], (8, 128))


def put_column(xf, dst, block):
    block = block.astype(F32)
    for g in range(3):
        xf[dst, g, 8:8 + ROWS, :] = block[:, g * 128:(g + 1) * 128]


def clear_pads(xf):
    zero = jnp.zeros((8, 128), F32)

    def body(i, _):
        for g in range(3):
            xf[i, g, 0:8, :] = zero
            xf[i, g, RP - 8:RP, :] = zero
        return 0
    lax.fori_loop(0, XC, body, 0)


def conv_cols(xf, tapb, g, j0, r0):
    accs = [None] * J
    for a in range(7):
        xs = [xf[j0 + i, g, pl.ds(r0 + 5 + a, 8), :] for i in range(J + 6)]
        for b in range(7):
            t = tapb[a * 7 + b, g]
            for j in range(J):
                p = t * xs[j + b]
                accs[j] = p if accs[j] is None else accs[j] + p
    return accs


def conv_block(xf, tapb, conv, jb):
    def gloop(g, _):
        def rloop(r, _):
            r0 = r * 8
            accs = conv_cols(xf, tapb, g, jb * J, r0)
            for j in range(J):
                conv[jb * J + j, g, pl.ds(pl.multiple_of(r0, 8), 8), :] = accs[j]
            return 0
        lax.fori_loop(0, 16, rloop, 0)
        return 0
    lax.fori_loop(0, 3, gloop, 0)


def back_block(df, tapb, cotb, dimg, jb):
    for g in range(3):
        ls = slice(g * 128, g * 128 + 128)

        def rloop(r, _):
            r0 = pl.multiple_of(r * 16, 16)
            lo = conv_cols(df, tapb, g, jb * J, r0)
            hi = conv_cols(df, tapb, g, jb * J, r0 + 8)
            for j in range(J):
                col = jb * J + j
                acc = jnp.concatenate([lo[j], hi[j]], axis=0) + cotb[col, pl.ds(r0, 16), ls].astype(F32)
                dimg[col, pl.ds(r0, 16), ls] = acc.astype(BF16)
            return 0
        lax.fori_loop(0, 8, rloop, 0)


def kernel_grads(xf, df, kacc, g):
    def aloop(a, _):
        def jloop(jb, accs):
            def rloop(r, accs):
                r0 = r * 8
                accs = list(accs)
                ds = [df[jb * J + 3 + j, g, pl.ds(pl.multiple_of(r0 + 8, 8), 8), :] for j in range(J)]
                xs = [xf[jb * J + i, g, pl.ds(r0 + 5 + a, 8), :] for i in range(J + 6)]
                for b in range(7):
                    p = ds[0] * xs[b]
                    for j in range(1, J):
                        p = p + ds[j] * xs[j + b]
                    accs[b] = accs[b] + p
                return tuple(accs)
            return lax.fori_loop(0, 16, rloop, accs, unroll=4)
        accs = lax.fori_loop(0, NC // J, jloop, tuple(jnp.zeros((8, 128), F32) for _ in range(7)))
        for b in range(7):
            kacc[a * 7 + b, g] = accs[b]
        return 0
    lax.fori_loop(0, 7, aloop, 0)


def part(x):
    return x.reshape(T // 8, 8, C).sum(0)


def mlp_step(s, conv, cotb, vecs, w1, w2, w1t, g1, g2, vacc, dcv):
    bias, gain, lbias, ls = vecs
    one_col = (lax.broadcasted_iota(jnp.int32, (T, 128), 1) == 0).astype(BF16)
    v = jnp.concatenate([conv[pl.ds(2 * s, 2), g].reshape(T, 128) for g in range(3)], axis=1) + bias
    v = v.astype(BF16).astype(F32)
    mean = jnp.sum(v, axis=1, keepdims=True) * (1.0 / C)
    cen = v - mean
    inv = lax.rsqrt(jnp.sum(cen * cen, axis=1, keepdims=True) * (1.0 / C) + 1e-6)
    nraw = cen * inv
    normed = jnp.concatenate([(nraw * gain + lbias).astype(BF16), one_col], axis=1)
    dmlp = (cotb[pl.ds(2 * s, 2)].reshape(T, C).astype(F32) * ls).astype(BF16)
    vacc[2] += part(dmlp.astype(F32))
    normed_t = normed.T
    dmlp_t = dmlp.T
    dn = jnp.zeros((T, C), F32)
    for f in range(FF // 256):
        sl = slice(f * 256, f * 256 + 256)
        pre = jnp.dot(normed, w1[:, sl], preferred_element_type=F32)
        dact = jnp.dot(dmlp, w2[:, sl], preferred_element_type=F32)
        act, slope = gelu_parts(pre)
        act = act.astype(BF16)
        dpre = (dact * slope).astype(BF16)
        g1[:, sl] += jnp.dot(normed_t, dpre, preferred_element_type=F32)
        g2[:, sl] += jnp.dot(dmlp_t, act, preferred_element_type=F32)
        dn += jnp.dot(dpre, w1t[f], preferred_element_type=F32)
    vacc[0] += part(dn * nraw)
    vacc[1] += part(dn)
    sc = dn * gain
    m1 = jnp.sum(sc, axis=1, keepdims=True) * (1.0 / C)
    m2 = jnp.sum(sc * nraw, axis=1, keepdims=True) * (1.0 / C)
    dc = (inv * (sc - m1 - nraw * m2)).astype(BF16)
    vacc[4] += part(dc.astype(F32))
    dcv[pl.ds(2 * s, 2)] = dc.reshape(2, ROWS, C)


def peers_of(me, coord, stride):
    return [me + (lax.rem(coord + o, 4) - coord) * stride for o in (1, 2, 3)]


def send(src, dst, sems, idx, dev):
    copy = pltpu.make_async_remote_copy(
        src_ref=src, dst_ref=dst, send_sem=sems[0].at[idx], recv_sem=sems[1].at[idx],
        device_id=(dev,), device_id_type=MESH)
    copy.start()
    return copy


def wait_all(copies):
    for copy in copies:
        copy.wait()


def kernel(widths, feat, cot, s1, s2, taps, vecs_ref,
           d_out, small_out, o1_out, o2_out,
           xsend, xmate, hsend, xhalo, csend, cmate,
           bx1, bx2, w1g, w2g, xf, df, tapb, tapf, conv, cotb, w1, w2, w1c, g1, g2, vacc, dcv,
           g1b, g2b, dsend, dhalo, rc1, rc2, c1, c2, rz1, ry2, t1, t2, ry1, rz2, p1, p2, rx1, rx2,
           kacc, cur, slots, dimg, rsend, rmate, ssem, rsem):
    me = lax.axis_index("strip")
    core = lax.rem(me, 2)
    y = lax.rem(me // 2, 4)
    x = lax.rem(me // 8, 4)
    z = me // 32
    xs, ys, zs = peers_of(me, x, 8), peers_of(me, y, 2), peers_of(me, z, 32)
    mate = me + 1 - 2 * core
    outer = lax.rem(me + 2 * core - 1 + N_DEV, N_DEV)
    sems = (ssem, rsem)
    is_a = core == 0
    wa, wb = widths[me - core], widths[me - core + 1]
    pair = wa + wb
    n0 = (pair + 1) // 2
    n = jnp.where(is_a, n0, pair - n0)
    p0 = jnp.where(is_a, 0, n0)
    mine = jnp.where(is_a, wa, wb)
    base = jnp.where(is_a, 0, wa)
    off9 = jnp.maximum(wa - 9, 0)
    off6 = jnp.maximum(wa - 6, 0)
    offr = jnp.maximum(n0 - 6, 0)

    barrier = pltpu.get_barrier_semaphore()
    for dev in xs + ys + zs + [mate, outer]:
        pl.semaphore_signal(barrier, inc=1, device_id=(dev,), device_id_type=MESH)

    s9, s6 = jnp.where(is_a, off9, 0), jnp.where(is_a, off6, 0)
    for i in range(9):
        xsend[i] = feat[s9 + i]
    for i in range(6):
        csend[i] = cot[s6 + i]
    h3 = jnp.where(is_a, 0, jnp.maximum(wb - 3, 0))
    for i in range(3):
        hsend[i] = feat[h3 + i]
    pl.semaphore_wait(barrier, 11)

    halo_in = [send(hsend, xhalo, sems, 0, outer), send(xsend, xmate, sems, 1, mate)]
    first = []
    for o in range(3):
        first.append(send(s1, bx1.at[x], sems, 2 + o, xs[o]))
        first.append(send(s2, bx2.at[x], sems, 5 + o, xs[o]))
    cot_in = send(csend, cmate, sems, 8, mate)
    bx1[x] = s1[...]
    bx2[x] = s2[...]
    fill_taps(taps, tapb, False)
    clear_pads(xf)
    clear_pads(df)
    wait_all(first)
    w1g[core, z, y] = jnp.concatenate([bx1[q].astype(F32)[:12] for q in range(4)], axis=0).astype(BF16)
    w2g[core, z, y] = jnp.concatenate([bx2[q].astype(F32)[:12] for q in range(4)], axis=0).astype(BF16)
    second = []
    for o in range(3):
        second.append(send(w1g.at[core, z, y], w1g.at[core, z, y], sems, 9 + o, ys[o]))
        second.append(send(w2g.at[core, z, y], w2g.at[core, z, y], sems, 12 + o, zs[o]))
    wait_all(halo_in)

    def place_x(i, _):
        p = p0 + i - 3
        q = p - base
        own = feat[jnp.clip(q, 0, CAP - 1)].astype(F32)
        other = xmate[jnp.clip(jnp.where(is_a, p - wa, p - off9), 0, 8)].astype(F32)
        edge = xhalo[jnp.clip(jnp.where(is_a, p + 3, p - pair), 0, 2)].astype(F32)
        is_own = (q >= 0) & (q < mine)
        is_edge = jnp.where(is_a, p < 0, p >= pair)
        gone = (i >= n + 6) | (is_edge & jnp.where(is_a, me == 0, me == N_DEV - 1))
        val = jnp.where(is_own, own, jnp.where(is_edge, edge, other))
        put_column(xf, i, jnp.where(gone, 0.0, val))
        return 0
    lax.fori_loop(0, XC, place_x, 0)
    wait_all(second)
    third = []
    for o in range(3):
        third.append(send(w1g.at[core, z], w1g.at[core, z], sems, 15 + o, zs[o]))
        third.append(send(w2g.at[core, :, y], w2g.at[core, :, y], sems, 18 + o, ys[o]))
    conv_block(xf, tapb, conv, 0)
    cot_in.wait()

    def place_cot(j, _):
        p = p0 + j
        q = p - base
        own = cot[jnp.clip(q, 0, CAP - 1)].astype(F32)
        other = cmate[jnp.clip(jnp.where(is_a, p - wa, p - off6), 0, 5)].astype(F32)
        val = jnp.where((q >= 0) & (q < mine), own, other)
        cotb[j] = jnp.where(j >= n, 0.0, val).astype(BF16)
        return 0
    lax.fori_loop(0, NC, place_cot, 0)
    conv_block(xf, tapb, conv, 1)
    wait_all(third)
    fourth = [send(w1g.at[core], w1g.at[core], sems, 21, mate), send(w2g.at[core], w2g.at[core], sems, 22, mate)]
    conv_block(xf, tapb, conv, 2)
    fill_taps(taps, tapf, True)
    vacc[...] = jnp.zeros_like(vacc)
    g1[...] = jnp.zeros_like(g1)
    g2[...] = jnp.zeros_like(g2)
    wait_all(fourth)

    w1full = w1g[...].reshape(FF, 512)
    w2full = w2g[...].reshape(FF, C)
    for f in range(FF // 256):
        sl = slice(f * 256, f * 256 + 256)
        w1[:, sl] = w1full[sl].T
        w2[:, sl] = w2full[sl].T
        w1c[f] = w1full[sl, :C]
    vecs = (vecs_ref[0:1, :], vecs_ref[1:2, :], vecs_ref[2:3, :], vecs_ref[3:4, :])

    def step(s, _):
        mlp_step(s, conv, cotb, vecs, w1, w2, w1c, g1, g2, vacc, dcv)
        return 0
    lax.fori_loop(0, NC // 2, step, 0)

    last_at = jnp.maximum(n - 3, 0)
    inner_at, outer_at = jnp.where(is_a, last_at, 0), jnp.where(is_a, 0, last_at)
    for i in range(3):
        dsend[0, i] = dcv[inner_at + i]
        dsend[1, i] = dcv[outer_at + i]
    halo_d = [send(dsend.at[0], dhalo.at[0], sems, 23, mate), send(dsend.at[1], dhalo.at[1], sems, 24, outer)]
    srow = jnp.zeros((8, C), F32)
    for q in range(4):
        b1 = g1[:, q * 384:(q + 1) * 384].T
        b2 = g2[:, q * 384:(q + 1) * 384].T
        srow += (b2 * w2full[q * 384:(q + 1) * 384].astype(F32)).reshape(48, 8, C).sum(0)
        for k in range(8):
            at = (q // 2, (q % 2) * 2 + k // 4, k % 4)
            g1b[at] = b1[k * 48:(k + 1) * 48].astype(BF16)
            g2b[at] = b2[k * 48:(k + 1) * 48].astype(BF16)
    vacc[3] = srow
    rs1 = [send(g1b.at[1 - core], rc1, sems, 25, mate), send(g2b.at[1 - core], rc2, sems, 26, mate)]

    def place_d(j, _):
        put_column(df, j + 3, dcv[j])
        return 0
    lax.fori_loop(0, NC, place_d, 0)
    kernel_grads(xf, df, kacc, 0)
    wait_all(rs1)

    def add_first(i, _):
        zi, yi = i // 4, lax.rem(i, 4)
        c1[zi, yi] = (g1b[core, zi, yi].astype(F32) + rc1[zi, yi].astype(F32)).astype(BF16)
        c2[zi, yi] = (g2b[core, zi, yi].astype(F32) + rc2[zi, yi].astype(F32)).astype(BF16)
        return 0
    lax.fori_loop(0, 16, add_first, 0)
    rs2 = []
    for o in range(3):
        rs2.append(send(c1.at[lax.rem(z + o + 1, 4)], rz1.at[o], sems, 27 + o, zs[o]))
        rs2.append(send(c2.at[:, lax.rem(y + o + 1, 4)], ry2.at[o], sems, 30 + o, ys[o]))
    kernel_grads(xf, df, kacc, 1)
    kernel_grads(xf, df, kacc, 2)

    def kout(i, _):
        cur[0, pl.ds(i, 1), :] = jnp.concatenate([jnp.sum(kacc[i, g], axis=0, keepdims=True) for g in range(3)], axis=1)
        return 0
    lax.fori_loop(0, 49, kout, 0)
    rows = [jnp.sum(vacc[i], axis=0, keepdims=True) for i in range(5)]
    cur[0, 49:56, :] = jnp.zeros((7, C), F32)
    cur[0, 56:64, :] = jnp.concatenate(rows + [jnp.zeros((3, C), F32)], axis=0)

    def sum_send(stage, at, group):
        return [send(cur.at[stage], slots.at[at + i], sems, 49 + at + i, dev) for i, dev in enumerate(group)]

    def sum_take(stage, at, copies):
        wait_all(copies)
        total = cur[stage]
        for i in range(len(copies)):
            total = total + slots[at + i]
        cur[stage + 1] = total

    sums = sum_send(0, 0, [mate])
    wait_all(halo_d)

    def place_edges(i, _):
        k = jnp.clip(i - n - 3, 0, 2)
        left = jnp.where(is_a, dhalo[1, jnp.clip(i, 0, 2)].astype(F32), dhalo[0, jnp.clip(i, 0, 2)].astype(F32))
        right = jnp.where(is_a, dhalo[0, k].astype(F32), dhalo[1, k].astype(F32))
        left = jnp.where(me == 0, 0.0, left)
        right = jnp.where((i >= n + 6) | (me == N_DEV - 1), 0.0, right)
        own = dcv[jnp.clip(i - 3, 0, NC - 1)].astype(F32)
        put_column(df, i, jnp.where(i < 3, left, jnp.where(i < n + 3, own, right)))
        return 0
    lax.fori_loop(0, XC, place_edges, 0)
    sum_take(0, 0, sums)
    sums = sum_send(1, 1, ys)
    back_block(df, tapf, cotb, dimg, 0)
    wait_all(rs2)

    def add_second(i, _):
        t1[i] = (c1[z, i].astype(F32) + rz1[0, i].astype(F32) + rz1[1, i].astype(F32) + rz1[2, i].astype(F32)).astype(BF16)
        t2[i] = (c2[i, y].astype(F32) + ry2[0, i].astype(F32) + ry2[1, i].astype(F32) + ry2[2, i].astype(F32)).astype(BF16)
        return 0
    lax.fori_loop(0, 4, add_second, 0)
    rs3 = []
    for o in range(3):
        rs3.append(send(t1.at[lax.rem(y + o + 1, 4)], ry1.at[o], sems, 33 + o, ys[o]))
        rs3.append(send(t2.at[lax.rem(z + o + 1, 4)], rz2.at[o], sems, 36 + o, zs[o]))
    sum_take(1, 1, sums)
    sums = sum_send(2, 4, zs)
    back_block(df, tapf, cotb, dimg, 1)
    wait_all(rs3)
    u1 = t1[y].astype(F32) + ry1[0].astype(F32) + ry1[1].astype(F32) + ry1[2].astype(F32)
    u2 = t2[z].astype(F32) + rz2[0].astype(F32) + rz2[1].astype(F32) + rz2[2].astype(F32)
    for q in range(4):
        p1[q, 0:12, :] = u1[q * 12:q * 12 + 12]
        p2[q, 0:12, :] = u2[q * 12:q * 12 + 12]
        p1[q, 12:16, :] = jnp.zeros((4, 512), F32)
        p2[q, 12:16, :] = jnp.zeros((4, C), F32)
    rs4 = []
    for o in range(3):
        q = lax.rem(x + o + 1, 4)
        rs4.append(send(p1.at[q], rx1.at[o], sems, 39 + o, xs[o]))
        rs4.append(send(p2.at[q], rx2.at[o], sems, 42 + o, xs[o]))
    sum_take(2, 4, sums)
    sums = sum_send(3, 7, xs)
    back_block(df, tapf, cotb, dimg, 2)
    sr = jnp.where(is_a, offr, 0)
    for i in range(6):
        rsend[i] = dimg[sr + i]
    back = send(rsend, rmate, sems, 45, mate)
    wait_all(rs4)
    o1_out[...] = (p1[x] + rx1[0] + rx1[1] + rx1[2]) * SCALE
    o2_out[...] = (p2[x] + rx2[0] + rx2[1] + rx2[2]) * SCALE
    sum_take(3, 7, sums)
    small_out[...] = cur[4] * SCALE
    back.wait()

    def place_out(s, _):
        p = base + s
        own = dimg[jnp.clip(p - p0, 0, NC - 1)]
        other = rmate[jnp.clip(jnp.where(is_a, p - n0, p - offr), 0, 5)]
        is_own = jnp.where(is_a, p < n0, p >= n0)
        val = jnp.where(is_own, own.astype(F32), other.astype(F32))
        d_out[s] = jnp.where(s >= mine, 0.0, val).astype(BF16)
        return 0
    lax.fori_loop(0, CAP, place_out, 0)


def fused(widths, feat, cot, s1, s2, taps, vecs):
    def v(*shape, dtype=BF16):
        return pltpu.VMEM(shape, dtype)
    return pl.pallas_call(
        kernel,
        out_shape=(
            jax.ShapeDtypeStruct((CAP, ROWS, C), BF16),
            jax.ShapeDtypeStruct((64, C), F32),
            jax.ShapeDtypeStruct((16, 512), F32),
            jax.ShapeDtypeStruct((16, C), F32),
        ),
        in_specs=[SMEM] + [VMEM] * 6,
        out_specs=[VMEM] * 4,
        scratch_shapes=[
            v(9, ROWS, C), v(9, ROWS, C), v(3, ROWS, C), v(3, ROWS, C), v(6, ROWS, C), v(6, ROWS, C),
            v(4, 16, 512), v(4, 16, C), v(2, 4, 4, 48, 512), v(2, 4, 4, 48, C),
            v(XC, 3, RP, 128, dtype=F32), v(XC, 3, RP, 128, dtype=F32),
            v(49, 3, 8, 128, dtype=F32), v(49, 3, 8, 128, dtype=F32),
            v(NC, 3, ROWS, 128, dtype=F32), v(NC, ROWS, C),
            v(512, FF), v(C, FF), v(FF // 256, 256, C), v(512, FF, dtype=F32), v(C, FF, dtype=F32),
            v(8, 8, C, dtype=F32), v(NC, ROWS, C),
            v(2, 4, 4, 48, 512), v(2, 4, 4, 48, C), v(2, 3, ROWS, C), v(2, 3, ROWS, C),
            v(4, 4, 48, 512), v(4, 4, 48, C), v(4, 4, 48, 512), v(4, 4, 48, C),
            v(3, 4, 48, 512), v(3, 4, 48, C), v(4, 48, 512), v(4, 48, C), v(3, 48, 512), v(3, 48, C),
            v(4, 16, 512, dtype=F32), v(4, 16, C, dtype=F32), v(3, 16, 512, dtype=F32), v(3, 16, C, dtype=F32),
            v(49, 3, 8, 128, dtype=F32), v(5, 64, C, dtype=F32), v(10, 64, C, dtype=F32),
            v(NC, ROWS, C), v(6, ROWS, C), v(6, ROWS, C),
            pltpu.SemaphoreType.DMA((59,)), pltpu.SemaphoreType.DMA((59,)),
        ],
        compiler_params=pltpu.CompilerParams(collective_id=0, has_side_effects=True, vmem_limit_bytes=60 * 2**20),
        name="block_back",
    )(widths, feat, cot, s1, s2, taps, vecs)


def local(features, grad_out, widths, dw_kernel, dw_bias, ln_gain, ln_bias,
          w_in, in_bias, w_out, out_bias, layer_scale):
    feat, cot = jnp.transpose(features, (1, 0, 2)), jnp.transpose(grad_out, (1, 0, 2))
    s1 = jnp.pad(jnp.concatenate([w_in.T, in_bias[:, None]], axis=1), ((0, 4), (0, 127)))
    s2 = jnp.pad(w_out, ((0, 4), (0, 0)))
    vecs = jnp.concatenate([dw_bias, ln_gain, ln_bias, layer_scale]).reshape(4, C).astype(F32)
    dimg, total, o1, o2 = fused(widths, feat, cot, s1, s2, dw_kernel, vecs)
    g_scale = (total[59] + out_bias.astype(F32) * total[58]) / layer_scale.astype(F32)
    return (jnp.transpose(dimg, (1, 0, 2)), total[:49], total[60], total[56], total[57],
            o1[:12, :C].T, o1[:12, C], o2[:12], total[58], g_scale)


def solution(mesh):
    wide = P(None, "strip", None)
    return jax.shard_map(
        local, mesh=mesh,
        in_specs=(wide, wide, P(), P(), P(), P(), P(), P(None, "strip"), P("strip"), P("strip", None), P(), P()),
        out_specs=(wide, P(), P(), P(), P(), P(None, "strip"), P("strip"), P("strip", None), P(), P()),
        check_vma=False)
```

```python
import math

import jax
import jax.numpy as jnp
from jax import lax
from jax.sharding import PartitionSpec as P
from jax.experimental import pallas as pl
from jax.experimental.pallas import tpu as pltpu

ROWS, C, FF, CAP = 128, 384, 1536, 15
N_DEV = 128
NC = 12
NW = 11
XC = NC + 6
RP = ROWS + 16
T = 2 * ROWS
F32, BF16 = jnp.float32, jnp.bfloat16
VMEM = pl.BlockSpec(memory_space=pltpu.VMEM)
SMEM = pl.BlockSpec(memory_space=pltpu.SMEM)
MESH = pl.DeviceIdType.MESH
SCALE = 1.0 / math.sqrt(ROWS * N_DEV * 5)


def gelu_parts(x):
    e = jnp.exp(x * x * -0.5)
    t = 1.0 / (1.0 + (0.3275911 * 0.7071067811865476) * jnp.abs(x))
    q = ((((0.5 * 1.061405429) * t - 0.5 * 1.453152027) * t + 0.5 * 1.421413741) * t - 0.5 * 0.284496736) * t + 0.5 * 0.254829592
    h = q * t * e
    cdf = jnp.where(x >= 0, 1.0 - h, h)
    slope = cdf + x * e * 0.3989422804014327
    return x * cdf, slope


def fill_taps(taps_ref, tapb, flip):
    for g in range(3):
        block = taps_ref[:, g * 128:(g + 1) * 128].astype(F32)
        for i in range(49):
            src = 48 - i if flip else i
            tapb[i, g] = jnp.broadcast_to(block[src:src + 1], (8, 128))


def put_column(xf, dst, block):
    block = block.astype(F32)
    for g in range(3):
        xf[dst, g, 8:8 + ROWS, :] = block[:, g * 128:(g + 1) * 128]


def clear_pads(xf):
    zero = jnp.zeros((8, 128), F32)

    def body(i, _):
        for g in range(3):
            xf[i, g, 0:8, :] = zero
            xf[i, g, RP - 8:RP, :] = zero
        return 0
    lax.fori_loop(0, XC, body, 0)


def conv_rows(xf, tapb, g, r0):
    def aloop(a, accs):
        accs = [list(part_) for part_ in accs]
        ts = [tapb[a * 7 + b, g] for b in range(7)]
        for i in range(NW + 6):
            for k in range(2):
                xv = xf[i, g, pl.ds(r0 + 8 * k + 5 + a, 8), :]
                for b in range(7):
                    if 0 <= i - b < NW:
                        accs[k][i - b] = accs[k][i - b] + ts[b] * xv
        return tuple(tuple(part_) for part_ in accs)
    zero = jnp.zeros((8, 128), F32)
    return lax.fori_loop(0, 7, aloop, ((zero,) * NW,) * 2)


def conv_group(xf, tapb, conv, g):
    def rloop(r, _):
        r0 = pl.multiple_of(r * 16, 16)
        lo, hi = conv_rows(xf, tapb, g, r0)
        for j in range(NW):
            conv[j, g, pl.ds(r0, 16), :] = jnp.concatenate([lo[j], hi[j]], axis=0)
        return 0
    lax.fori_loop(0, 8, rloop, 0)


def back_group(df, tapb, cotb, dimg, g):
    ls = slice(g * 128, g * 128 + 128)

    def rloop(r, _):
        r0 = pl.multiple_of(r * 16, 16)
        lo, hi = conv_rows(df, tapb, g, r0)
        for j in range(NW):
            acc = jnp.concatenate([lo[j], hi[j]], axis=0) + cotb[j, pl.ds(r0, 16), ls].astype(F32)
            dimg[j, pl.ds(r0, 16), ls] = acc.astype(BF16)
        return 0
    lax.fori_loop(0, 8, rloop, 0)


def kernel_grads(xf, df, kacc, g):
    def aloop(a, _):
        def rloop(r, accs):
            r0 = r * 8
            accs = list(accs)
            ds = [df[3 + j, g, pl.ds(pl.multiple_of(r0 + 8, 8), 8), :] for j in range(NW)]
            for i in range(NW + 6):
                xv = xf[i, g, pl.ds(r0 + 5 + a, 8), :]
                for b in range(7):
                    if 0 <= i - b < NW:
                        accs[b] = accs[b] + ds[i - b] * xv
            return tuple(accs)
        accs = lax.fori_loop(0, 16, rloop, tuple(jnp.zeros((8, 128), F32) for _ in range(7)), unroll=2)
        for b in range(7):
            kacc[a * 7 + b, g] = accs[b]
        return 0
    lax.fori_loop(0, 7, aloop, 0)


def part(x):
    return x.reshape(T // 8, 8, C).sum(0)


def mlp_step(s, conv, cotb, vecs, w1, w2, w1t, g1, g2, vacc, dcv):
    bias, gain, lbias, ls = vecs
    one_col = (lax.broadcasted_iota(jnp.int32, (T, 128), 1) == 0).astype(BF16)
    v = jnp.concatenate([conv[pl.ds(2 * s, 2), g].reshape(T, 128) for g in range(3)], axis=1) + bias
    v = v.astype(BF16).astype(F32)
    mean = jnp.sum(v, axis=1, keepdims=True) * (1.0 / C)
    cen = v - mean
    inv = lax.rsqrt(jnp.sum(cen * cen, axis=1, keepdims=True) * (1.0 / C) + 1e-6)
    nraw = cen * inv
    normed = jnp.concatenate([(nraw * gain + lbias).astype(BF16), one_col], axis=1)
    dmlp = (cotb[pl.ds(2 * s, 2)].reshape(T, C).astype(F32) * ls).astype(BF16)
    vacc[2] += part(dmlp.astype(F32))
    normed_t = normed.T
    dmlp_t = dmlp.T
    blocks = [slice(f * 256, f * 256 + 256) for f in range(FF // 256)]

    def front(sl):
        return (jnp.dot(normed, w1[:, sl], preferred_element_type=F32),
                jnp.dot(dmlp, w2[:, sl], preferred_element_type=F32))
    acts, dpres = [], []
    ahead = front(blocks[0])
    for f in range(len(blocks)):
        pre, dact = ahead
        if f + 1 < len(blocks):
            ahead = front(blocks[f + 1])
        act, slope = gelu_parts(pre)
        acts.append(act.astype(BF16))
        dpres.append((dact * slope).astype(BF16))
    dn = jnp.dot(jnp.concatenate(dpres, axis=1), w1t[...], preferred_element_type=F32)
    for sl, act, dpre in zip(blocks, acts, dpres):
        g1[:, sl] += jnp.dot(normed_t, dpre, preferred_element_type=F32)
        g2[:, sl] += jnp.dot(dmlp_t, act, preferred_element_type=F32)
    vacc[0] += part(dn * nraw)
    vacc[1] += part(dn)
    sc = dn * gain
    m1 = jnp.sum(sc, axis=1, keepdims=True) * (1.0 / C)
    m2 = jnp.sum(sc * nraw, axis=1, keepdims=True) * (1.0 / C)
    dc = (inv * (sc - m1 - nraw * m2)).astype(BF16)
    vacc[4] += part(dc.astype(F32))
    dcv[pl.ds(2 * s, 2)] = dc.reshape(2, ROWS, C)


def peers_of(me, coord, stride):
    return [me + (lax.rem(coord + o, 4) - coord) * stride for o in (1, 2, 3)]


def send(src, dst, sems, idx, dev):
    copy = pltpu.make_async_remote_copy(
        src_ref=src, dst_ref=dst, send_sem=sems[0].at[idx], recv_sem=sems[1].at[idx],
        device_id=(dev,), device_id_type=MESH)
    copy.start()
    return copy


def wait_all(copies):
    for copy in copies:
        copy.wait()


def kernel(widths, feat, cot, w_in_t, in_bias, w_out, taps, dw_bias, ln_gain, ln_bias, layer_scale,
           dimg_out, rmate_out, small_out, o1_out, o2_out,
           s1, s2, sbias,
           xsend, xmate, hsend, xhalo, csend, cmate,
           bx1, bx2, w1g, w2g, xf, df, tapb, tapf, conv, cotb, w1, w2, w1c, g1, g2, vacc, dcv,
           g1b, g2b, dsend, dhalo, rc1, rc2, c1, c2, rz1, ry2, t1, t2, ry1, rz2, p1, p2, rx1, rx2,
           kacc, krow, cur, mslot, part_sum, slots, total, dimg, rsend, rmate, ssem, rsem):
    me = lax.axis_index("strip")
    core = lax.rem(me, 2)
    y = lax.rem(me // 2, 4)
    x = lax.rem(me // 8, 4)
    z = me // 32
    xs, ys, zs = peers_of(me, x, 8), peers_of(me, y, 2), peers_of(me, z, 32)
    mate = me + 1 - 2 * core
    outer = lax.rem(me + 2 * core - 1 + N_DEV, N_DEV)
    sems = (ssem, rsem)
    is_a = core == 0
    wa, wb = widths[me - core], widths[me - core + 1]
    pair = wa + wb
    n0 = (pair + 1) // 2
    n = jnp.where(is_a, n0, pair - n0)
    p0 = jnp.where(is_a, 0, n0)
    mine = jnp.where(is_a, wa, wb)
    base = jnp.where(is_a, 0, wa)
    off9 = jnp.maximum(wa - 9, 0)
    off6 = jnp.maximum(wa - 6, 0)
    offr = jnp.maximum(n0 - 6, 0)

    barrier = pltpu.get_barrier_semaphore()
    for dev in xs + ys + zs + [mate, outer]:
        pl.semaphore_signal(barrier, inc=1, device_id=(dev,), device_id_type=MESH)

    s9, s6 = jnp.where(is_a, off9, 0), jnp.where(is_a, off6, 0)
    for i in range(9):
        xsend[i] = feat[s9 + i]
    for i in range(6):
        csend[i] = cot[s6 + i]
    h3 = jnp.where(is_a, 0, jnp.maximum(wb - 3, 0))
    for i in range(3):
        hsend[i] = feat[h3 + i]
    sbias[...] = jnp.zeros_like(sbias)
    sbias[0:1, 0:12] = in_bias[...].astype(F32).reshape(1, 12)
    s1[:, C:512] = sbias[...].T[0:16].astype(BF16)
    pad4 = jnp.zeros((4, C), F32)
    s1[:, 0:C] = jnp.concatenate([w_in_t[...].astype(F32), pad4], axis=0).astype(BF16)
    s2[...] = jnp.concatenate([w_out[...].astype(F32), pad4], axis=0).astype(BF16)
    pl.semaphore_wait(barrier, 11)

    halo_in = [send(hsend, xhalo, sems, 0, outer), send(xsend, xmate, sems, 1, mate)]
    first = []
    for o in range(3):
        first.append(send(s1, bx1.at[x], sems, 2 + o, xs[o]))
        first.append(send(s2, bx2.at[x], sems, 5 + o, xs[o]))
    cot_in = send(csend, cmate, sems, 8, mate)
    bx1[x] = s1[...]
    bx2[x] = s2[...]
    fill_taps(taps, tapb, False)
    clear_pads(xf)
    clear_pads(df)
    wait_all(first)
    w1g[core, z, y] = jnp.concatenate([bx1[q].astype(F32)[:12] for q in range(4)], axis=0).astype(BF16)
    w2g[core, z, y] = jnp.concatenate([bx2[q].astype(F32)[:12] for q in range(4)], axis=0).astype(BF16)
    second = []
    for o in range(3):
        second.append(send(w1g.at[core, z, y], w1g.at[core, z, y], sems, 9 + o, ys[o]))
        second.append(send(w2g.at[core, z, y], w2g.at[core, z, y], sems, 12 + o, zs[o]))
    wait_all(halo_in)

    def place_x(i, _):
        p = p0 + i - 3
        q = p - base
        own = feat[jnp.clip(q, 0, CAP - 1)].astype(F32)
        other = xmate[jnp.clip(jnp.where(is_a, p - wa, p - off9), 0, 8)].astype(F32)
        edge = xhalo[jnp.clip(jnp.where(is_a, p + 3, p - pair), 0, 2)].astype(F32)
        is_own = (q >= 0) & (q < mine)
        is_edge = jnp.where(is_a, p < 0, p >= pair)
        gone = (i >= n + 6) | (is_edge & jnp.where(is_a, me == 0, me == N_DEV - 1))
        val = jnp.where(is_own, own, jnp.where(is_edge, edge, other))
        put_column(xf, i, jnp.where(gone, 0.0, val))
        return 0
    lax.fori_loop(0, XC, place_x, 0)
    wait_all(second)
    third1, third2 = [], []
    for o in range(3):
        third1.append(send(w1g.at[core, z], w1g.at[core, z], sems, 15 + o, zs[o]))
        third2.append(send(w2g.at[core, :, y], w2g.at[core, :, y], sems, 18 + o, ys[o]))
    fourth = [send(w1g.at[core, z], w1g.at[core, z], sems, 21, mate),
              send(w2g.at[core, :, y], w2g.at[core, :, y], sems, 22, mate)]
    conv_group(xf, tapb, conv, 0)
    cot_in.wait()

    def place_cot(j, _):
        p = p0 + j
        q = p - base
        own = cot[jnp.clip(q, 0, CAP - 1)].astype(F32)
        other = cmate[jnp.clip(jnp.where(is_a, p - wa, p - off6), 0, 5)].astype(F32)
        val = jnp.where((q >= 0) & (q < mine), own, other)
        cotb[j] = jnp.where(j >= n, 0.0, val).astype(BF16)
        return 0
    lax.fori_loop(0, NC, place_cot, 0)
    conv_group(xf, tapb, conv, 1)
    for o in range(3):
        zb, yb = lax.rem(z + 3 - o, 4), lax.rem(y + 3 - o, 4)
        third1[o].wait()
        fourth.append(send(w1g.at[core, zb], w1g.at[core, zb], sems, 59 + o, mate))
        third2[o].wait()
        fourth.append(send(w2g.at[core, :, yb], w2g.at[core, :, yb], sems, 62 + o, mate))
    conv_group(xf, tapb, conv, 2)
    conv[NC - 1] = jnp.zeros((3, ROWS, 128), F32)
    fill_taps(taps, tapf, True)
    vacc[...] = jnp.zeros_like(vacc)
    g1[...] = jnp.zeros_like(g1)
    g2[...] = jnp.zeros_like(g2)
    wait_all(fourth)
    w1full = w1g[...].reshape(FF, 512)
    w2full = w2g[...].reshape(FF, C)
    for f in range(FF // 256):
        sl = slice(f * 256, f * 256 + 256)
        w1[:, sl] = w1full[sl].T
        w2[:, sl] = w2full[sl].T
        w1c[sl, :] = w1full[sl, :C]
    vecs = tuple(ref[...].astype(F32).reshape(1, C) for ref in (dw_bias, ln_gain, ln_bias, layer_scale))

    def step(s, _):
        mlp_step(s, conv, cotb, vecs, w1, w2, w1c, g1, g2, vacc, dcv)
        return 0
    lax.fori_loop(0, NC // 2, step, 0)

    last_at = jnp.maximum(n - 3, 0)
    inner_at, outer_at = jnp.where(is_a, last_at, 0), jnp.where(is_a, 0, last_at)
    for i in range(3):
        dsend[0, i] = dcv[inner_at + i]
        dsend[1, i] = dcv[outer_at + i]
    halo_d = [send(dsend.at[0], dhalo.at[0], sems, 23, mate), send(dsend.at[1], dhalo.at[1], sems, 24, outer)]
    srow = jnp.zeros((8, C), F32)
    rs1 = []
    for h in range(2):
        half = 1 - core if h == 0 else core
        for q in range(2):
            at = pl.ds(pl.multiple_of(half * 768 + q * 384, 128), 384)
            b1 = g1[:, at].T
            b2 = g2[:, at].T
            wrow = w2g[half, pl.ds(2 * q, 2)].reshape(384, C)
            srow += (b2 * wrow.astype(F32)).reshape(48, 8, C).sum(0)
            for k in range(8):
                g1b[half, 2 * q + k // 4, k % 4] = b1[k * 48:(k + 1) * 48].astype(BF16)
                g2b[half, 2 * q + k // 4, k % 4] = b2[k * 48:(k + 1) * 48].astype(BF16)
        if h == 0:
            rs1 = [send(g1b.at[half], rc1, sems, 25, mate), send(g2b.at[half], rc2, sems, 26, mate)]
    vacc[3] = srow

    def place_d(j, _):
        put_column(df, j + 3, dcv[j])
        return 0
    lax.fori_loop(0, NC, place_d, 0)
    kernel_grads(xf, df, kacc, 0)
    wait_all(rs1)

    def add_first(i, _):
        zi, yi = i // 4, lax.rem(i, 4)
        c1[zi, yi] = (g1b[core, zi, yi].astype(F32) + rc1[zi, yi].astype(F32)).astype(BF16)
        c2[zi, yi] = (g2b[core, zi, yi].astype(F32) + rc2[zi, yi].astype(F32)).astype(BF16)
        return 0
    lax.fori_loop(0, 16, add_first, 0)
    rs2 = []
    for o in range(3):
        rs2.append(send(c1.at[lax.rem(z + o + 1, 4)], rz1.at[o], sems, 27 + o, zs[o]))
        rs2.append(send(c2.at[:, lax.rem(y + o + 1, 4)], ry2.at[o], sems, 30 + o, ys[o]))
    kernel_grads(xf, df, kacc, 1)
    kernel_grads(xf, df, kacc, 2)

    def kout(i, _):
        krow[pl.ds(i, 1), :] = jnp.concatenate([jnp.sum(kacc[i, g], axis=0, keepdims=True) for g in range(3)], axis=1)
        return 0
    lax.fori_loop(0, 49, kout, 0)
    rows = [jnp.sum(vacc[i], axis=0, keepdims=True) for i in range(5)]
    krow[49:56, :] = jnp.zeros((7, C), F32)
    krow[56:64, :] = jnp.concatenate(rows + [jnp.zeros((3, C), F32)], axis=0)
    cur[...] = krow[...].reshape(2, 2, 16, C)

    def sum_send(stage, groups):
        copies = []
        for h, group in enumerate(groups):
            for i, dev in enumerate(group):
                k = stage * 6 + h * 3 + i
                copies.append(send(part_sum.at[stage, h], slots.at[k], sems, 65 + k, dev))
        return copies

    def sum_take(stage, copies):
        wait_all(copies)
        for h in range(2):
            k = stage * 6 + h * 3
            part_sum[stage + 1, h] = part_sum[stage, h] + slots[k] + slots[k + 1] + slots[k + 2]

    first_sum = send(cur.at[1 - core], mslot, sems, 46, mate)
    first_sum.wait()
    for h in range(2):
        part_sum[0, h] = cur[core, h] + mslot[h]
    sums = sum_send(0, (ys, zs))
    wait_all(halo_d)

    def place_edges(i, _):
        k = jnp.clip(i - n - 3, 0, 2)
        left = jnp.where(is_a, dhalo[1, jnp.clip(i, 0, 2)].astype(F32), dhalo[0, jnp.clip(i, 0, 2)].astype(F32))
        right = jnp.where(is_a, dhalo[0, k].astype(F32), dhalo[1, k].astype(F32))
        left = jnp.where(me == 0, 0.0, left)
        right = jnp.where((i >= n + 6) | (me == N_DEV - 1), 0.0, right)
        own = dcv[jnp.clip(i - 3, 0, NC - 1)].astype(F32)
        put_column(df, i, jnp.where(i < 3, left, jnp.where(i < n + 3, own, right)))
        return 0
    lax.fori_loop(0, XC, place_edges, 0)
    back_group(df, tapf, cotb, dimg, 0)
    wait_all(rs2)

    def add_second(i, _):
        t1[i] = (c1[z, i].astype(F32) + rz1[0, i].astype(F32) + rz1[1, i].astype(F32) + rz1[2, i].astype(F32)).astype(BF16)
        t2[i] = (c2[i, y].astype(F32) + ry2[0, i].astype(F32) + ry2[1, i].astype(F32) + ry2[2, i].astype(F32)).astype(BF16)
        return 0
    lax.fori_loop(0, 4, add_second, 0)
    rs3 = []
    for o in range(3):
        rs3.append(send(t1.at[lax.rem(y + o + 1, 4)], ry1.at[o], sems, 33 + o, ys[o]))
        rs3.append(send(t2.at[lax.rem(z + o + 1, 4)], rz2.at[o], sems, 36 + o, zs[o]))
    sum_take(0, sums)
    sums = sum_send(1, (zs, xs))
    back_group(df, tapf, cotb, dimg, 1)
    wait_all(rs3)
    u1 = t1[y].astype(F32) + ry1[0].astype(F32) + ry1[1].astype(F32) + ry1[2].astype(F32)
    u2 = t2[z].astype(F32) + rz2[0].astype(F32) + rz2[1].astype(F32) + rz2[2].astype(F32)
    for q in range(4):
        p1[q, 0:12, :] = u1[q * 12:q * 12 + 12]
        p2[q, 0:12, :] = u2[q * 12:q * 12 + 12]
        p1[q, 12:16, :] = jnp.zeros((4, 512), F32)
        p2[q, 12:16, :] = jnp.zeros((4, C), F32)
    rs4 = []
    for o in range(3):
        q = lax.rem(x + o + 1, 4)
        rs4.append(send(p1.at[q], rx1.at[o], sems, 39 + o, xs[o]))
        rs4.append(send(p2.at[q], rx2.at[o], sems, 42 + o, xs[o]))
    sum_take(1, sums)
    sums = sum_send(2, (xs, ys))
    back_group(df, tapf, cotb, dimg, 2)
    sr = jnp.where(is_a, offr, 0)
    for i in range(6):
        rsend[i] = dimg[sr + i]
    back = send(rsend, rmate, sems, 45, mate)
    wait_all(rs4)
    o1_out[...] = (p1[x] + rx1[0] + rx1[1] + rx1[2]) * SCALE
    o2_out[...] = (p2[x] + rx2[0] + rx2[1] + rx2[2]) * SCALE
    sum_take(2, sums)
    total[core] = part_sum[3]
    last = send(total.at[core], total.at[core], sems, 47, mate)
    dimg_out[...] = dimg[...]
    last.wait()
    small_out[...] = total[...].reshape(64, C) * SCALE
    back.wait()
    rmate_out[...] = rmate[...]


def finish_kernel(widths, place, dimg, rmate, total, o1, o2, out_bias, layer_scale,
                  d_out, g_kernel, g_bias, g_gain, g_lbias, g_win, g_ibias, g_wout, g_obias, g_scale):
    me = place[0]
    core = lax.rem(me, 2)
    is_a = core == 0
    wa, wb = widths[me - core], widths[me - core + 1]
    n0 = (wa + wb + 1) // 2
    p0 = jnp.where(is_a, 0, n0)
    mine = jnp.where(is_a, wa, wb)
    base = jnp.where(is_a, 0, wa)
    offr = jnp.maximum(n0 - 6, 0)

    def place_out(s, _):
        p = base + s
        own = dimg[jnp.clip(p - p0, 0, NC - 1)]
        other = rmate[jnp.clip(jnp.where(is_a, p - n0, p - offr), 0, 5)]
        is_own = jnp.where(is_a, p < n0, p >= n0)
        val = jnp.where(is_own, own.astype(F32), other.astype(F32))
        d_out[s] = jnp.where(s >= mine, 0.0, val).astype(BF16)
        return 0
    lax.fori_loop(0, CAP, place_out, 0)
    g_kernel[...] = total[0:49]

    def row(i):
        return total[i:i + 1, :]
    g_gain[...] = row(56).reshape(C)
    g_lbias[...] = row(57).reshape(C)
    g_obias[...] = row(58).reshape(C)
    g_bias[...] = row(60).reshape(C)
    ls, ob = layer_scale[...].astype(F32).reshape(1, C), out_bias[...].astype(F32).reshape(1, C)
    g_scale[...] = ((row(59) + ob * row(58)) / ls).reshape(C)
    g_win[...] = o1[0:12, 0:C]
    g_ibias[...] = o1[:, C:512].T[0:1, 0:12].reshape(12)
    g_wout[...] = o2[0:12]


def finish(widths, place, *args):
    def f(*shape, dtype=F32):
        return jax.ShapeDtypeStruct(shape, dtype)
    return pl.pallas_call(
        finish_kernel,
        out_shape=(f(CAP, ROWS, C, dtype=BF16), f(49, C), f(C), f(C), f(C), f(12, C), f(12), f(12, C), f(C), f(C)),
        in_specs=[SMEM] * 2 + [VMEM] * 7,
        out_specs=[VMEM] * 10,
        compiler_params=pltpu.CompilerParams(vmem_limit_bytes=24 * 2**20),
        name="place_results",
    )(widths, place, *args)


def fused(*args):
    def v(*shape, dtype=BF16):
        return pltpu.VMEM(shape, dtype)
    return pl.pallas_call(
        kernel,
        out_shape=(
            jax.ShapeDtypeStruct((NC, ROWS, C), BF16),
            jax.ShapeDtypeStruct((6, ROWS, C), BF16),
            jax.ShapeDtypeStruct((64, C), F32),
            jax.ShapeDtypeStruct((16, 512), F32),
            jax.ShapeDtypeStruct((16, C), F32),
        ),
        in_specs=[SMEM] + [VMEM] * 10,
        out_specs=[VMEM] * 5,
        scratch_shapes=[
            v(16, 512), v(16, C), v(128, 128, dtype=F32),
            v(9, ROWS, C), v(9, ROWS, C), v(3, ROWS, C), v(3, ROWS, C), v(6, ROWS, C), v(6, ROWS, C),
            v(4, 16, 512), v(4, 16, C), v(2, 4, 4, 48, 512), v(2, 4, 4, 48, C),
            v(XC, 3, RP, 128, dtype=F32), v(XC, 3, RP, 128, dtype=F32),
            v(49, 3, 8, 128, dtype=F32), v(49, 3, 8, 128, dtype=F32),
            v(NC, 3, ROWS, 128, dtype=F32), v(NC, ROWS, C),
            v(512, FF), v(C, FF), v(FF, C), v(512, FF, dtype=F32), v(C, FF, dtype=F32),
            v(8, 8, C, dtype=F32), v(NC, ROWS, C),
            v(2, 4, 4, 48, 512), v(2, 4, 4, 48, C), v(2, 3, ROWS, C), v(2, 3, ROWS, C),
            v(4, 4, 48, 512), v(4, 4, 48, C), v(4, 4, 48, 512), v(4, 4, 48, C),
            v(3, 4, 48, 512), v(3, 4, 48, C), v(4, 48, 512), v(4, 48, C), v(3, 48, 512), v(3, 48, C),
            v(4, 16, 512, dtype=F32), v(4, 16, C, dtype=F32), v(3, 16, 512, dtype=F32), v(3, 16, C, dtype=F32),
            v(49, 3, 8, 128, dtype=F32), v(64, C, dtype=F32), v(2, 2, 16, C, dtype=F32), v(2, 16, C, dtype=F32),
            v(4, 2, 16, C, dtype=F32), v(18, 16, C, dtype=F32), v(2, 2, 16, C, dtype=F32),
            v(NC, ROWS, C), v(6, ROWS, C), v(6, ROWS, C),
            pltpu.SemaphoreType.DMA((83,)), pltpu.SemaphoreType.DMA((83,)),
        ],
        compiler_params=pltpu.CompilerParams(collective_id=0, has_side_effects=True, vmem_limit_bytes=60 * 2**20),
        name="block_back",
    )(*args)


def local(features, grad_out, widths, dw_kernel, dw_bias, ln_gain, ln_bias,
          w_in, in_bias, w_out, out_bias, layer_scale):
    feat, cot = jnp.transpose(features, (1, 0, 2)), jnp.transpose(grad_out, (1, 0, 2))
    place = lax.axis_index("strip").reshape(1)
    dimg, rmate, total, o1, o2 = fused(widths, feat, cot, w_in.T, in_bias, w_out, dw_kernel,
                                       dw_bias, ln_gain, ln_bias, layer_scale)
    outs = finish(widths, place, dimg, rmate, total, o1, o2, out_bias, layer_scale)
    return (jnp.transpose(outs[0], (1, 0, 2)),) + tuple(outs[1:5]) + (outs[5].T,) + tuple(outs[6:])


def solution(mesh):
    wide = P(None, "strip", None)
    return jax.shard_map(
        local, mesh=mesh,
        in_specs=(wide, wide, P(), P(), P(), P(), P(), P(None, "strip"), P("strip"), P("strip", None), P(), P()),
        out_specs=(wide, P(), P(), P(), P(), P(None, "strip"), P("strip"), P("strip", None), P(), P()),
        check_vma=False)
```

```python
import math

import jax
import jax.numpy as jnp
from jax import lax
from jax.sharding import PartitionSpec as P
from jax.experimental import pallas as pl
from jax.experimental.pallas import tpu as pltpu

ROWS, C, FF, CAP = 128, 384, 1536, 15
N_DEV = 128
NC = 12
NW = 11
XC = NC + 6
RP = ROWS + 16
T = 2 * ROWS
TOK = NC * ROWS
F32, BF16 = jnp.float32, jnp.bfloat16
VMEM = pl.BlockSpec(memory_space=pltpu.VMEM)
SMEM = pl.BlockSpec(memory_space=pltpu.SMEM)
MESH = pl.DeviceIdType.MESH
SCALE = 1.0 / math.sqrt(ROWS * N_DEV * 5)


def gelu_parts(x):
    e = jnp.exp(x * x * -0.5)
    t = 1.0 / (1.0 + (0.3275911 * 0.7071067811865476) * jnp.abs(x))
    q = ((((0.5 * 1.061405429) * t - 0.5 * 1.453152027) * t + 0.5 * 1.421413741) * t - 0.5 * 0.284496736) * t + 0.5 * 0.254829592
    h = q * t * e
    cdf = jnp.where(x >= 0, 1.0 - h, h)
    slope = cdf + x * e * 0.3989422804014327
    return x * cdf, slope


def fill_taps(taps_ref, tapb, flip):
    for g in range(3):
        block = taps_ref[:, g * 128:(g + 1) * 128].astype(F32)
        for i in range(49):
            src = 48 - i if flip else i
            tapb[i, g] = jnp.broadcast_to(block[src:src + 1], (8, 128))


def put_column(xf, dst, block):
    block = block.astype(F32)
    for g in range(3):
        xf[dst, g, 8:8 + ROWS, :] = block[:, g * 128:(g + 1) * 128]


def clear_pads(xf):
    zero = jnp.zeros((8, 128), F32)

    def body(i, _):
        for g in range(3):
            xf[i, g, 0:8, :] = zero
            xf[i, g, RP - 8:RP, :] = zero
        return 0
    lax.fori_loop(0, XC, body, 0)


def conv_rows(xf, tapb, g, r0):
    def aloop(a, accs):
        accs = [list(part_) for part_ in accs]
        ts = [tapb[a * 7 + b, g] for b in range(7)]
        for i in range(NW + 6):
            for k in range(2):
                xv = xf[i, g, pl.ds(r0 + 8 * k + 5 + a, 8), :]
                for b in range(7):
                    if 0 <= i - b < NW:
                        accs[k][i - b] = accs[k][i - b] + ts[b] * xv
        return tuple(tuple(part_) for part_ in accs)
    zero = jnp.zeros((8, 128), F32)
    return lax.fori_loop(0, 7, aloop, ((zero,) * NW,) * 2)


def conv_group(xf, tapb, conv, g):
    def rloop(r, _):
        r0 = pl.multiple_of(r * 16, 16)
        lo, hi = conv_rows(xf, tapb, g, r0)
        for j in range(NW):
            conv[j, g, pl.ds(r0, 16), :] = jnp.concatenate([lo[j], hi[j]], axis=0)
        return 0
    lax.fori_loop(0, 8, rloop, 0)


def back_group(df, tapb, cotb, dimg, g):
    ls = slice(g * 128, g * 128 + 128)

    def rloop(r, _):
        r0 = pl.multiple_of(r * 16, 16)
        lo, hi = conv_rows(df, tapb, g, r0)
        for j in range(NW):
            acc = jnp.concatenate([lo[j], hi[j]], axis=0) + cotb[j, pl.ds(r0, 16), ls].astype(F32)
            dimg[j, pl.ds(r0, 16), ls] = acc.astype(BF16)
        return 0
    lax.fori_loop(0, 8, rloop, 0)


def kernel_grads(xf, df, kacc, g):
    def aloop(a, _):
        def rloop(r, accs):
            r0 = r * 8
            accs = list(accs)
            ds = [df[3 + j, g, pl.ds(pl.multiple_of(r0 + 8, 8), 8), :] for j in range(NW)]
            for i in range(NW + 6):
                xv = xf[i, g, pl.ds(r0 + 5 + a, 8), :]
                for b in range(7):
                    if 0 <= i - b < NW:
                        accs[b] = accs[b] + ds[i - b] * xv
            return tuple(accs)
        accs = lax.fori_loop(0, 16, rloop, tuple(jnp.zeros((8, 128), F32) for _ in range(7)), unroll=2)
        for b in range(7):
            kacc[a * 7 + b, g] = accs[b]
        return 0
    lax.fori_loop(0, 7, aloop, 0)


def part(x):
    return x.reshape(T // 8, 8, C).sum(0)


def norm_step(s, conv, cotb, vecs, nrm, nrm_t, dm, dm_t, nraw_s, inv_s, vacc):
    bias, gain, lbias, ls = vecs
    at = pl.ds(pl.multiple_of(s * T, T), T)
    one_col = (lax.broadcasted_iota(jnp.int32, (T, 128), 1) == 0).astype(BF16)
    v = jnp.concatenate([conv[pl.ds(2 * s, 2), g].reshape(T, 128) for g in range(3)], axis=1) + bias
    v = v.astype(BF16).astype(F32)
    mean = jnp.sum(v, axis=1, keepdims=True) * (1.0 / C)
    cen = v - mean
    inv = lax.rsqrt(jnp.sum(cen * cen, axis=1, keepdims=True) * (1.0 / C) + 1e-6)
    nraw = cen * inv
    normed = jnp.concatenate([(nraw * gain + lbias).astype(BF16), one_col], axis=1)
    dmlp = (cotb[pl.ds(2 * s, 2)].reshape(T, C).astype(F32) * ls).astype(BF16)
    vacc[2] += part(dmlp.astype(F32))
    nrm[at, :] = normed
    nrm_t[:, at] = normed.T
    dm[at, :] = dmlp
    dm_t[:, at] = dmlp.T
    nraw_s[at, :] = nraw
    inv_s[at, :] = jnp.broadcast_to(inv, (T, 128))


def hidden_block(first, nrm, dm, wa, wb, wrows, act_s, dpre_s, dn_s):
    ats = [slice(k * T, k * T + T) for k in range(TOK // T)]

    def front(at):
        return (jnp.dot(nrm[at, :], wa[...], preferred_element_type=F32),
                jnp.dot(dm[at, :], wb[...], preferred_element_type=F32))
    ahead = front(ats[0])
    for i, at in enumerate(ats):
        pre, dact = ahead
        if i + 1 < len(ats):
            ahead = front(ats[i + 1])
        act, slope = gelu_parts(pre)
        act_s[at, :] = act.astype(BF16)
        dpre = (dact * slope).astype(BF16)
        dpre_s[at, :] = dpre
        dn = jnp.dot(dpre, wrows[...], preferred_element_type=F32)
        dn_s[at, :] = dn if first else dn_s[at, :] + dn


def denorm_step(s, dn_s, nraw_s, inv_s, gain, vacc, dcv):
    at = pl.ds(pl.multiple_of(s * T, T), T)
    dn, nraw, inv = dn_s[at, :], nraw_s[at, :], inv_s[at, 0:1]
    vacc[0] += part(dn * nraw)
    vacc[1] += part(dn)
    sc = dn * gain
    m1 = jnp.sum(sc, axis=1, keepdims=True) * (1.0 / C)
    m2 = jnp.sum(sc * nraw, axis=1, keepdims=True) * (1.0 / C)
    dc = (inv * (sc - m1 - nraw * m2)).astype(BF16)
    vacc[4] += part(dc.astype(F32))
    dcv[pl.ds(2 * s, 2)] = dc.reshape(2, ROWS, C)


def peers_of(me, coord, stride):
    return [me + (lax.rem(coord + o, 4) - coord) * stride for o in (1, 2, 3)]


def send(src, dst, sems, idx, dev):
    copy = pltpu.make_async_remote_copy(
        src_ref=src, dst_ref=dst, send_sem=sems[0].at[idx], recv_sem=sems[1].at[idx],
        device_id=(dev,), device_id_type=MESH)
    copy.start()
    return copy


def wait_all(copies):
    for copy in copies:
        copy.wait()


def kernel(widths, feat_any, cot_any, w_in_t, in_bias, w_out, taps, dw_bias, ln_gain, ln_bias, layer_scale,
           dimg_out, rmate_out, small_out, o1_out, o2_out,
           feat, cot, s1, s2, sbias,
           xsend, xmate, hsend, xhalo, csend, cmate,
           bx1, bx2, w1g, w2g, xf, df, tapb, tapf, conv, cotb, nrm, nrm_t, dm, dm_t, nraw_s, inv_s, dn_s,
           act_a, dpre_a, act_b, dpre_b, mwa, mwb, wr, vacc, dcv,
           g1b, g2b, dsend, dhalo, rc1, rc2, c1, c2, rz1, ry2, t1, t2, ry1, rz2, p1, p2, rx1, rx2,
           kacc, krow, cur, mslot, part_sum, slots, total, dimg, rsend, rmate, ssem, rsem, lsem):
    me = lax.axis_index("strip")
    core = lax.rem(me, 2)
    y = lax.rem(me // 2, 4)
    x = lax.rem(me // 8, 4)
    z = me // 32
    xs, ys, zs = peers_of(me, x, 8), peers_of(me, y, 2), peers_of(me, z, 32)
    mate = me + 1 - 2 * core
    outer = lax.rem(me + 2 * core - 1 + N_DEV, N_DEV)
    sems = (ssem, rsem)
    is_a = core == 0
    wa, wb = widths[me - core], widths[me - core + 1]
    pair = wa + wb
    n0 = (pair + 1) // 2
    n = jnp.where(is_a, n0, pair - n0)
    p0 = jnp.where(is_a, 0, n0)
    mine = jnp.where(is_a, wa, wb)
    base = jnp.where(is_a, 0, wa)
    off9 = jnp.maximum(wa - 9, 0)
    off6 = jnp.maximum(wa - 6, 0)
    offr = jnp.maximum(n0 - 6, 0)

    barrier = pltpu.get_barrier_semaphore()
    for dev in xs + ys + zs + [mate, outer]:
        pl.semaphore_signal(barrier, inc=1, device_id=(dev,), device_id_type=MESH)

    loads = [pltpu.make_async_copy(feat_any, feat, lsem.at[0]), pltpu.make_async_copy(cot_any, cot, lsem.at[1])]
    for load in loads:
        load.start()
    s9, s6 = jnp.where(is_a, off9, 0), jnp.where(is_a, off6, 0)
    h3 = jnp.where(is_a, 0, jnp.maximum(wb - 3, 0))
    sbias[...] = jnp.zeros_like(sbias)
    sbias[0:1, 0:12] = in_bias[...].astype(F32).reshape(1, 12)
    s1[:, C:512] = sbias[...].T[0:16].astype(BF16)
    pad4 = jnp.zeros((4, C), F32)
    s1[:, 0:C] = jnp.concatenate([w_in_t[...].astype(F32), pad4], axis=0).astype(BF16)
    s2[...] = jnp.concatenate([w_out[...].astype(F32), pad4], axis=0).astype(BF16)
    pl.semaphore_wait(barrier, 11)

    first = []
    for o in range(3):
        first.append(send(s1, bx1.at[x], sems, 2 + o, xs[o]))
        first.append(send(s2, bx2.at[x], sems, 5 + o, xs[o]))
    bx1[x] = s1[...]
    bx2[x] = s2[...]
    loads[0].wait()
    for i in range(3):
        hsend[i] = feat[h3 + i]
    halo_in = [send(hsend, xhalo, sems, 0, outer)]
    for i in range(9):
        xsend[i] = feat[s9 + i]
    halo_in.append(send(xsend, xmate, sems, 1, mate))
    wait_all(first)
    for ch in range(3):
        rows4 = slice(ch * 4, ch * 4 + 4)
        w1g[core, ch, z, y] = jnp.concatenate([bx1[q].astype(F32)[rows4] for q in range(4)], axis=0).astype(BF16)
        w2g[core, ch, z, y] = jnp.concatenate([bx2[q].astype(F32)[rows4] for q in range(4)], axis=0).astype(BF16)
    second = []
    for o in range(3):
        second.append(send(w1g.at[core, :, z, y], w1g.at[core, :, z, y], sems, 9 + o, ys[o]))
        second.append(send(w2g.at[core, :, z, y], w2g.at[core, :, z, y], sems, 12 + o, zs[o]))
    loads[1].wait()
    for i in range(6):
        csend[i] = cot[s6 + i]
    cot_in = send(csend, cmate, sems, 8, mate)
    fill_taps(taps, tapb, False)
    clear_pads(xf)
    clear_pads(df)
    wait_all(second)
    third = []
    for ch in range(3):
        copies = []
        for o in range(3):
            copies.append(send(w1g.at[core, ch, z], w1g.at[core, ch, z], sems, 83 + ch * 6 + o, zs[o]))
            copies.append(send(w2g.at[core, ch, :, y], w2g.at[core, ch, :, y], sems, 83 + ch * 6 + 3 + o, ys[o]))
        third.append(copies)

    def pass_on(ch):
        wait_all(third[ch])
        return [send(w1g.at[core, ch], w1g.at[core, ch], sems, 101 + 2 * ch, mate),
                send(w2g.at[core, ch], w2g.at[core, ch], sems, 102 + 2 * ch, mate)]
    wait_all(halo_in)

    def place_x(i, _):
        p = p0 + i - 3
        q = p - base
        own = feat[jnp.clip(q, 0, CAP - 1)].astype(F32)
        other = xmate[jnp.clip(jnp.where(is_a, p - wa, p - off9), 0, 8)].astype(F32)
        edge = xhalo[jnp.clip(jnp.where(is_a, p + 3, p - pair), 0, 2)].astype(F32)
        is_own = (q >= 0) & (q < mine)
        is_edge = jnp.where(is_a, p < 0, p >= pair)
        gone = (i >= n + 6) | (is_edge & jnp.where(is_a, me == 0, me == N_DEV - 1))
        val = jnp.where(is_own, own, jnp.where(is_edge, edge, other))
        put_column(xf, i, jnp.where(gone, 0.0, val))
        return 0
    lax.fori_loop(0, XC, place_x, 0)
    conv_group(xf, tapb, conv, 0)
    cot_in.wait()

    def place_cot(j, _):
        p = p0 + j
        q = p - base
        own = cot[jnp.clip(q, 0, CAP - 1)].astype(F32)
        other = cmate[jnp.clip(jnp.where(is_a, p - wa, p - off6), 0, 5)].astype(F32)
        val = jnp.where((q >= 0) & (q < mine), own, other)
        cotb[j] = jnp.where(j >= n, 0.0, val).astype(BF16)
        return 0
    lax.fori_loop(0, NC, place_cot, 0)
    conv_group(xf, tapb, conv, 1)
    passed = [pass_on(0)]
    conv_group(xf, tapb, conv, 2)
    conv[NC - 1] = jnp.zeros((3, ROWS, 128), F32)
    vacc[...] = jnp.zeros_like(vacc)
    vecs = tuple(ref[...].astype(F32).reshape(1, C) for ref in (dw_bias, ln_gain, ln_bias, layer_scale))

    def before(s, _):
        norm_step(s, conv, cotb, vecs, nrm, nrm_t, dm, dm_t, nraw_s, inv_s, vacc)
        return 0
    lax.fori_loop(0, NC // 2, before, 0)

    sums_w = [jnp.zeros((8, C), F32)]
    rs1, rs2 = {}, []

    def weight_grads(ch, own_half, act_s, dpre_s):
        half = core if own_half else 1 - core
        b1 = jnp.dot(nrm_t[...], dpre_s[...], preferred_element_type=F32).T
        b2 = jnp.dot(dm_t[...], act_s[...], preferred_element_type=F32).T
        sums_w[0] += (b2 * w2g[half, ch].reshape(256, C).astype(F32)).reshape(32, 8, C).sum(0)
        to1, to2 = (c1, c2) if own_half else (g1b, g2b)
        to1[ch] = b1.astype(BF16).reshape(4, 4, 16, 512)
        to2[ch] = b2.astype(BF16).reshape(4, 4, 16, C)

    def give(ch):
        rs1[ch] = [send(g1b.at[ch], rc1.at[ch], sems, 125 + 2 * ch, mate),
                   send(g2b.at[ch], rc2.at[ch], sems, 126 + 2 * ch, mate)]

    def join(ch):
        wait_all(rs1[ch])
        for q in range(4):
            c1[ch, q] = (c1[ch, q].astype(F32) + rc1[ch, q].astype(F32)).astype(BF16)
            c2[ch, q] = (c2[ch, q].astype(F32) + rc2[ch, q].astype(F32)).astype(BF16)
        copies = []
        for o in range(3):
            k = 107 + ch * 6 + o
            copies.append(send(c1.at[ch, lax.rem(z + o + 1, 4)], rz1.at[ch, o], sems, k, zs[o]))
            copies.append(send(c2.at[ch, :, lax.rem(y + o + 1, 4)], ry2.at[ch, o], sems, k + 3, ys[o]))
        rs2.append(copies)

    order = [(0, True), (0, False), (1, False), (1, True), (2, False), (2, True)]
    hold = ((act_a, dpre_a), (act_b, dpre_b))
    for turn, (ch, own_half) in enumerate(order):
        half = core if own_half else 1 - core
        if turn in (1, 2):
            passed.append(pass_on(turn))
        if not own_half:
            wait_all(passed[ch])
        mwa[...] = w1g[half, ch].reshape(256, 512).T
        mwb[...] = w2g[half, ch].reshape(256, C).T
        wr[...] = w1g[half, ch].reshape(256, 512)[:, 0:C]
        if turn > 0:
            weight_grads(*order[turn - 1], *hold[(turn - 1) % 2])
        hidden_block(turn == 0, nrm, dm, mwa, mwb, wr, *hold[turn % 2], dn_s)
        if turn > 0 and not order[turn - 1][1]:
            give(order[turn - 1][0])
        if turn in (3, 4):
            join(turn - 3)
    weight_grads(*order[5], *hold[1])
    join(2)
    srow = sums_w[0]
    vacc[3] = srow

    def after(s, _):
        denorm_step(s, dn_s, nraw_s, inv_s, vecs[1], vacc, dcv)
        return 0
    lax.fori_loop(0, NC // 2, after, 0)

    last_at = jnp.maximum(n - 3, 0)
    inner_at, outer_at = jnp.where(is_a, last_at, 0), jnp.where(is_a, 0, last_at)
    for i in range(3):
        dsend[0, i] = dcv[inner_at + i]
        dsend[1, i] = dcv[outer_at + i]
    halo_d = [send(dsend.at[0], dhalo.at[0], sems, 23, mate), send(dsend.at[1], dhalo.at[1], sems, 24, outer)]
    def place_d(j, _):
        put_column(df, j + 3, dcv[j])
        return 0
    lax.fori_loop(0, NC, place_d, 0)
    kernel_grads(xf, df, kacc, 0)
    fill_taps(taps, tapf, True)
    kernel_grads(xf, df, kacc, 1)
    for copies in rs2:
        wait_all(copies)
    rs3 = []

    def add_second(i, _):
        ch, q = i // 4, lax.rem(i, 4)
        t1[ch, q] = (c1[ch, z, q].astype(F32) + rz1[ch, 0, q].astype(F32) + rz1[ch, 1, q].astype(F32)
                     + rz1[ch, 2, q].astype(F32)).astype(BF16)
        t2[ch, q] = (c2[ch, q, y].astype(F32) + ry2[ch, 0, q].astype(F32) + ry2[ch, 1, q].astype(F32)
                     + ry2[ch, 2, q].astype(F32)).astype(BF16)
        return 0
    lax.fori_loop(0, 12, add_second, 0)
    for o in range(3):
        rs3.append(send(t1.at[:, lax.rem(y + o + 1, 4)], ry1.at[o], sems, 33 + o, ys[o]))
        rs3.append(send(t2.at[:, lax.rem(z + o + 1, 4)], rz2.at[o], sems, 36 + o, zs[o]))
    kernel_grads(xf, df, kacc, 2)

    def kout(i, _):
        krow[pl.ds(i, 1), :] = jnp.concatenate([jnp.sum(kacc[i, g], axis=0, keepdims=True) for g in range(3)], axis=1)
        return 0
    lax.fori_loop(0, 49, kout, 0)
    rows = [jnp.sum(vacc[i], axis=0, keepdims=True) for i in range(5)]
    krow[49:56, :] = jnp.zeros((7, C), F32)
    krow[56:64, :] = jnp.concatenate(rows + [jnp.zeros((3, C), F32)], axis=0)
    cur[...] = krow[...].reshape(2, 2, 16, C)

    def sum_send(stage, groups):
        copies = []
        for h, group in enumerate(groups):
            for i, dev in enumerate(group):
                k = stage * 6 + h * 3 + i
                copies.append(send(part_sum.at[stage, h], slots.at[k], sems, 65 + k, dev))
        return copies

    def sum_take(stage, copies):
        wait_all(copies)
        for h in range(2):
            k = stage * 6 + h * 3
            part_sum[stage + 1, h] = part_sum[stage, h] + slots[k] + slots[k + 1] + slots[k + 2]

    first_sum = send(cur.at[1 - core], mslot, sems, 46, mate)
    first_sum.wait()
    for h in range(2):
        part_sum[0, h] = cur[core, h] + mslot[h]
    sums = sum_send(0, (ys, zs))
    wait_all(rs3)
    for ch in range(3):
        u1 = (t1[ch, y].astype(F32) + ry1[0, ch].astype(F32)) + (ry1[1, ch].astype(F32) + ry1[2, ch].astype(F32))
        u2 = (t2[ch, z].astype(F32) + rz2[0, ch].astype(F32)) + (rz2[1, ch].astype(F32) + rz2[2, ch].astype(F32))
        for q in range(4):
            p1[q, ch * 4:ch * 4 + 4, :] = u1[q * 4:q * 4 + 4]
            p2[q, ch * 4:ch * 4 + 4, :] = u2[q * 4:q * 4 + 4]
    for q in range(4):
        p1[q, 12:16, :] = jnp.zeros((4, 512), F32)
        p2[q, 12:16, :] = jnp.zeros((4, C), F32)
    rs4 = []
    for o in range(3):
        q = lax.rem(x + o + 1, 4)
        rs4.append(send(p1.at[q], rx1.at[o], sems, 39 + o, xs[o]))
        rs4.append(send(p2.at[q], rx2.at[o], sems, 42 + o, xs[o]))
    wait_all(halo_d)

    def place_edges(i, _):
        k = jnp.clip(i - n - 3, 0, 2)
        left = jnp.where(is_a, dhalo[1, jnp.clip(i, 0, 2)].astype(F32), dhalo[0, jnp.clip(i, 0, 2)].astype(F32))
        right = jnp.where(is_a, dhalo[0, k].astype(F32), dhalo[1, k].astype(F32))
        left = jnp.where(me == 0, 0.0, left)
        right = jnp.where((i >= n + 6) | (me == N_DEV - 1), 0.0, right)
        own = dcv[jnp.clip(i - 3, 0, NC - 1)].astype(F32)
        put_column(df, i, jnp.where(i < 3, left, jnp.where(i < n + 3, own, right)))
        return 0
    lax.fori_loop(0, XC, place_edges, 0)
    back_group(df, tapf, cotb, dimg, 0)
    sum_take(0, sums)
    sums = sum_send(1, (zs, xs))
    back_group(df, tapf, cotb, dimg, 1)
    sum_take(1, sums)
    sums = sum_send(2, (xs, ys))
    back_group(df, tapf, cotb, dimg, 2)
    sr = jnp.where(is_a, offr, 0)
    for i in range(6):
        rsend[i] = dimg[sr + i]
    back = send(rsend, rmate, sems, 45, mate)
    wait_all(rs4)
    o1_out[...] = (p1[x] + rx1[0] + rx1[1] + rx1[2]) * SCALE
    o2_out[...] = (p2[x] + rx2[0] + rx2[1] + rx2[2]) * SCALE
    sum_take(2, sums)
    total[core] = part_sum[3]
    last = send(total.at[core], total.at[core], sems, 47, mate)
    dimg_out[...] = dimg[...]
    last.wait()
    small_out[...] = total[...].reshape(64, C) * SCALE
    back.wait()
    rmate_out[...] = rmate[...]


def finish_kernel(widths, place, dimg, rmate, total, o1, o2, out_bias, layer_scale,
                  d_out, g_kernel, g_bias, g_gain, g_lbias, g_win, g_ibias, g_wout, g_obias, g_scale):
    me = place[0]
    core = lax.rem(me, 2)
    is_a = core == 0
    wa, wb = widths[me - core], widths[me - core + 1]
    n0 = (wa + wb + 1) // 2
    p0 = jnp.where(is_a, 0, n0)
    mine = jnp.where(is_a, wa, wb)
    base = jnp.where(is_a, 0, wa)
    offr = jnp.maximum(n0 - 6, 0)

    def place_out(s, _):
        p = base + s
        own = dimg[jnp.clip(p - p0, 0, NC - 1)]
        other = rmate[jnp.clip(jnp.where(is_a, p - n0, p - offr), 0, 5)]
        is_own = jnp.where(is_a, p < n0, p >= n0)
        val = jnp.where(is_own, own.astype(F32), other.astype(F32))
        d_out[s] = jnp.where(s >= mine, 0.0, val).astype(BF16)
        return 0
    lax.fori_loop(0, CAP, place_out, 0)
    g_kernel[...] = total[0:49]

    def row(i):
        return total[i:i + 1, :]
    g_gain[...] = row(56).reshape(C)
    g_lbias[...] = row(57).reshape(C)
    g_obias[...] = row(58).reshape(C)
    g_bias[...] = row(60).reshape(C)
    ls, ob = layer_scale[...].astype(F32).reshape(1, C), out_bias[...].astype(F32).reshape(1, C)
    g_scale[...] = ((row(59) + ob * row(58)) / ls).reshape(C)
    g_win[...] = o1[0:12, 0:C]
    g_ibias[...] = o1[:, C:512].T[0:1, 0:12].reshape(12)
    g_wout[...] = o2[0:12]


def finish(widths, place, *args):
    def f(*shape, dtype=F32):
        return jax.ShapeDtypeStruct(shape, dtype)
    return pl.pallas_call(
        finish_kernel,
        out_shape=(f(CAP, ROWS, C, dtype=BF16), f(49, C), f(C), f(C), f(C), f(12, C), f(12), f(12, C), f(C), f(C)),
        in_specs=[SMEM] * 2 + [VMEM] * 7,
        out_specs=[VMEM] * 10,
        compiler_params=pltpu.CompilerParams(vmem_limit_bytes=60 * 2**20),
        name="place_results",
    )(widths, place, *args)


def fused(*args):
    def v(*shape, dtype=BF16):
        return pltpu.VMEM(shape, dtype)
    return pl.pallas_call(
        kernel,
        out_shape=(
            jax.ShapeDtypeStruct((NC, ROWS, C), BF16),
            jax.ShapeDtypeStruct((6, ROWS, C), BF16),
            jax.ShapeDtypeStruct((64, C), F32),
            jax.ShapeDtypeStruct((16, 512), F32),
            jax.ShapeDtypeStruct((16, C), F32),
        ),
        in_specs=[SMEM] + [pl.BlockSpec(memory_space=pl.ANY)] * 2 + [VMEM] * 8,
        out_specs=[VMEM] * 5,
        scratch_shapes=[
            v(CAP, ROWS, C), v(CAP, ROWS, C), v(16, 512), v(16, C), v(128, 128, dtype=F32),
            v(9, ROWS, C), v(9, ROWS, C), v(3, ROWS, C), v(3, ROWS, C), v(6, ROWS, C), v(6, ROWS, C),
            v(4, 16, 512), v(4, 16, C), v(2, 3, 4, 4, 16, 512), v(2, 3, 4, 4, 16, C),
            v(XC, 3, RP, 128, dtype=F32), v(XC, 3, RP, 128, dtype=F32),
            v(49, 3, 8, 128, dtype=F32), v(49, 3, 8, 128, dtype=F32),
            v(NC, 3, ROWS, 128, dtype=F32), v(NC, ROWS, C),
            v(TOK, 512), v(512, TOK), v(TOK, C), v(C, TOK), v(TOK, C, dtype=F32), v(TOK, 128, dtype=F32), v(TOK, C, dtype=F32),
            v(TOK, 256), v(TOK, 256), v(TOK, 256), v(TOK, 256), v(512, 256), v(C, 256), v(256, C),
            v(8, 8, C, dtype=F32), v(NC, ROWS, C),
            v(3, 4, 4, 16, 512), v(3, 4, 4, 16, C), v(2, 3, ROWS, C), v(2, 3, ROWS, C),
            v(3, 4, 4, 16, 512), v(3, 4, 4, 16, C), v(3, 4, 4, 16, 512), v(3, 4, 4, 16, C),
            v(3, 3, 4, 16, 512), v(3, 3, 4, 16, C), v(3, 4, 16, 512), v(3, 4, 16, C), v(3, 3, 16, 512), v(3, 3, 16, C),
            v(4, 16, 512, dtype=F32), v(4, 16, C, dtype=F32), v(3, 16, 512, dtype=F32), v(3, 16, C, dtype=F32),
            v(49, 3, 8, 128, dtype=F32), v(64, C, dtype=F32), v(2, 2, 16, C, dtype=F32), v(2, 16, C, dtype=F32),
            v(4, 2, 16, C, dtype=F32), v(18, 16, C, dtype=F32), v(2, 2, 16, C, dtype=F32),
            v(NC, ROWS, C), v(6, ROWS, C), v(6, ROWS, C),
            pltpu.SemaphoreType.DMA((131,)), pltpu.SemaphoreType.DMA((131,)), pltpu.SemaphoreType.DMA((2,)),
        ],
        compiler_params=pltpu.CompilerParams(collective_id=0, has_side_effects=True, vmem_limit_bytes=60 * 2**20),
        name="block_back",
    )(*args)


def local(features, grad_out, widths, dw_kernel, dw_bias, ln_gain, ln_bias,
          w_in, in_bias, w_out, out_bias, layer_scale):
    feat, cot = jnp.transpose(features, (1, 0, 2)), jnp.transpose(grad_out, (1, 0, 2))
    place = lax.axis_index("strip").reshape(1)
    dimg, rmate, total, o1, o2 = fused(widths, feat, cot, w_in.T, in_bias, w_out, dw_kernel,
                                       dw_bias, ln_gain, ln_bias, layer_scale)
    outs = finish(widths, place, dimg, rmate, total, o1, o2, out_bias, layer_scale)
    return (jnp.transpose(outs[0], (1, 0, 2)),) + tuple(outs[1:5]) + (outs[5].T,) + tuple(outs[6:])


def solution(mesh):
    wide = P(None, "strip", None)
    return jax.shard_map(
        local, mesh=mesh,
        in_specs=(wide, wide, P(), P(), P(), P(), P(), P(None, "strip"), P("strip"), P("strip", None), P(), P()),
        out_specs=(wide, P(), P(), P(), P(), P(None, "strip"), P("strip"), P("strip", None), P(), P()),
        check_vma=False)
```

```python
import math

import jax
import jax.numpy as jnp
from jax import lax
from jax.sharding import PartitionSpec as P
from jax.experimental import pallas as pl
from jax.experimental.pallas import tpu as pltpu

ROWS, C, FF, CAP = 128, 384, 1536, 15
N_DEV = 128
NC = 12
NW = 11
XC = NC + 6
RP = ROWS + 16
T = 2 * ROWS
TOK = NC * ROWS
F32, BF16 = jnp.float32, jnp.bfloat16
VMEM = pl.BlockSpec(memory_space=pltpu.VMEM)
SMEM = pl.BlockSpec(memory_space=pltpu.SMEM)
MESH = pl.DeviceIdType.MESH
SCALE = 1.0 / math.sqrt(ROWS * N_DEV * 5)


def gelu_parts(x):
    e = jnp.exp(x * x * -0.5)
    t = 1.0 / (1.0 + (0.3275911 * 0.7071067811865476) * jnp.abs(x))
    q = ((((0.5 * 1.061405429) * t - 0.5 * 1.453152027) * t + 0.5 * 1.421413741) * t - 0.5 * 0.284496736) * t + 0.5 * 0.254829592
    h = q * t * e
    cdf = jnp.where(x >= 0, 1.0 - h, h)
    slope = cdf + x * e * 0.3989422804014327
    return x * cdf, slope


def fill_taps(taps_ref, tapb, flip):
    for g in range(3):
        block = taps_ref[:, g * 128:(g + 1) * 128].astype(F32)
        for i in range(49):
            src = 48 - i if flip else i
            tapb[i, g] = jnp.broadcast_to(block[src:src + 1], (8, 128))


def put_column(xf, dst, block):
    block = block.astype(F32)
    for g in range(3):
        xf[dst, g, 8:8 + ROWS, :] = block[:, g * 128:(g + 1) * 128]


def clear_pads(xf):
    zero = jnp.zeros((8, 128), F32)

    def body(i, _):
        for g in range(3):
            xf[i, g, 0:8, :] = zero
            xf[i, g, RP - 8:RP, :] = zero
        return 0
    lax.fori_loop(0, XC, body, 0)


def conv_rows(xf, tapb, g, r0):
    def aloop(a, accs):
        accs = [list(part_) for part_ in accs]
        ts = [tapb[a * 7 + b, g] for b in range(7)]
        for i in range(NW + 6):
            for k in range(2):
                xv = xf[i, g, pl.ds(r0 + 8 * k + 5 + a, 8), :]
                for b in range(7):
                    if 0 <= i - b < NW:
                        accs[k][i - b] = accs[k][i - b] + ts[b] * xv
        return tuple(tuple(part_) for part_ in accs)
    zero = jnp.zeros((8, 128), F32)
    return lax.fori_loop(0, 7, aloop, ((zero,) * NW,) * 2)


def conv_group(xf, tapb, conv, g):
    def rloop(r, _):
        r0 = pl.multiple_of(r * 16, 16)
        lo, hi = conv_rows(xf, tapb, g, r0)
        for j in range(NW):
            conv[j, g, pl.ds(r0, 16), :] = jnp.concatenate([lo[j], hi[j]], axis=0)
        return 0
    lax.fori_loop(0, 8, rloop, 0)


def back_group(df, tapb, cotb, dimg, g):
    ls = slice(g * 128, g * 128 + 128)

    def rloop(r, _):
        r0 = pl.multiple_of(r * 16, 16)
        lo, hi = conv_rows(df, tapb, g, r0)
        for j in range(NW):
            acc = jnp.concatenate([lo[j], hi[j]], axis=0) + cotb[j, pl.ds(r0, 16), ls].astype(F32)
            dimg[j, pl.ds(r0, 16), ls] = acc.astype(BF16)
        return 0
    lax.fori_loop(0, 8, rloop, 0)


def kernel_grads(xf, df, kacc, g):
    def aloop(a, _):
        def rloop(r, accs):
            r0 = r * 8
            accs = list(accs)
            ds = [df[3 + j, g, pl.ds(pl.multiple_of(r0 + 8, 8), 8), :] for j in range(NW)]
            for i in range(NW + 6):
                xv = xf[i, g, pl.ds(r0 + 5 + a, 8), :]
                for b in range(7):
                    if 0 <= i - b < NW:
                        accs[b] = accs[b] + ds[i - b] * xv
            return tuple(accs)
        accs = lax.fori_loop(0, 16, rloop, tuple(jnp.zeros((8, 128), F32) for _ in range(7)), unroll=2)
        for b in range(7):
            kacc[a * 7 + b, g] = accs[b]
        return 0
    lax.fori_loop(0, 7, aloop, 0)


def part(x):
    return x.reshape(T // 8, 8, C).sum(0)


def norm_step(s, conv, cotb, vecs, nrm, nrm_t, dm, dm_t, nraw_s, inv_s, vacc):
    bias, gain, lbias, ls = vecs
    at = pl.ds(pl.multiple_of(s * T, T), T)
    one_col = (lax.broadcasted_iota(jnp.int32, (T, 128), 1) == 0).astype(BF16)
    v = jnp.concatenate([conv[pl.ds(2 * s, 2), g].reshape(T, 128) for g in range(3)], axis=1) + bias
    v = v.astype(BF16).astype(F32)
    mean = jnp.sum(v, axis=1, keepdims=True) * (1.0 / C)
    cen = v - mean
    inv = lax.rsqrt(jnp.sum(cen * cen, axis=1, keepdims=True) * (1.0 / C) + 1e-6)
    nraw = cen * inv
    normed = jnp.concatenate([(nraw * gain + lbias).astype(BF16), one_col], axis=1)
    dmlp = (cotb[pl.ds(2 * s, 2)].reshape(T, C).astype(F32) * ls).astype(BF16)
    vacc[2] += part(dmlp.astype(F32))
    nrm[at, :] = normed
    nrm_t[:, at] = normed.T
    dm[at, :] = dmlp
    dm_t[:, at] = dmlp.T
    nraw_s[at, :] = nraw
    inv_s[at, :] = jnp.broadcast_to(inv, (T, 128))


def hidden_block(first, nrm, dm, wa, wb, wrows, act_s, dpre_s, dn_s):
    ats = [slice(k * T, k * T + T) for k in range(TOK // T)]

    def front(at):
        return (jnp.dot(nrm[at, :], wa[...], preferred_element_type=F32),
                jnp.dot(dm[at, :], wb[...], preferred_element_type=F32))
    ahead = front(ats[0])
    for i, at in enumerate(ats):
        pre, dact = ahead
        if i + 1 < len(ats):
            ahead = front(ats[i + 1])
        act, slope = gelu_parts(pre)
        act_s[at, :] = act.astype(BF16)
        dpre = (dact * slope).astype(BF16)
        dpre_s[at, :] = dpre
        dn = jnp.dot(dpre, wrows[...], preferred_element_type=F32)
        dn_s[at, :] = dn if first else dn_s[at, :] + dn


def denorm_step(s, dn_s, nraw_s, inv_s, gain, vacc, dcv):
    at = pl.ds(pl.multiple_of(s * T, T), T)
    dn, nraw, inv = dn_s[at, :], nraw_s[at, :], inv_s[at, 0:1]
    vacc[0] += part(dn * nraw)
    vacc[1] += part(dn)
    sc = dn * gain
    m1 = jnp.sum(sc, axis=1, keepdims=True) * (1.0 / C)
    m2 = jnp.sum(sc * nraw, axis=1, keepdims=True) * (1.0 / C)
    dc = (inv * (sc - m1 - nraw * m2)).astype(BF16)
    vacc[4] += part(dc.astype(F32))
    dcv[pl.ds(2 * s, 2)] = dc.reshape(2, ROWS, C)


def peers_of(me, coord, stride):
    return [me + (lax.rem(coord + o, 4) - coord) * stride for o in (1, 2, 3)]


def send(src, dst, sems, idx, dev):
    copy = pltpu.make_async_remote_copy(
        src_ref=src, dst_ref=dst, send_sem=sems[0].at[idx], recv_sem=sems[1].at[idx],
        device_id=(dev,), device_id_type=MESH)
    copy.start()
    return copy


def wait_all(copies):
    for copy in copies:
        copy.wait()


def kernel(widths, feat_any, cot_any, w_in_t, in_bias, w_out, taps, dw_bias, ln_gain, ln_bias, layer_scale,
           dimg_out, rmate_out, small_out, o1_out, o2_out,
           feat, cot, s1, s2, sbias,
           xsend, xmate, hsend, xhalo_a, xhalo_b, xhalo_c, csend, cmate,
           bx1, bx2, w1g, w2g, xf, df, tapb, tapf, conv, cotb, nrm, nrm_t, dm, dm_t, nraw_s, inv_s, dn_s,
           act_a, dpre_a, act_b, dpre_b, mwa, mwb, wr, vacc, dcv,
           g1b, g2b, dsend, dhalo, rc1, rc2, c1, c2, rz1, ry2, t1, t2, ry1, rz2, p1, p2, rx1, rx2,
           kacc, krow, cur, mslot, part_sum, slots, total, dimg, rsend, rmate, ssem, rsem, lsem):
    me = lax.axis_index("strip")
    core = lax.rem(me, 2)
    y = lax.rem(me // 2, 4)
    x = lax.rem(me // 8, 4)
    z = me // 32
    xs, ys, zs = peers_of(me, x, 8), peers_of(me, y, 2), peers_of(me, z, 32)
    mate = me + 1 - 2 * core
    outer = lax.rem(me + 2 * core - 1 + N_DEV, N_DEV)
    sems = (ssem, rsem)
    is_a = core == 0
    wa, wb = widths[me - core], widths[me - core + 1]
    pair = wa + wb
    n0 = (pair + 1) // 2
    n = jnp.where(is_a, n0, pair - n0)
    p0 = jnp.where(is_a, 0, n0)
    mine = jnp.where(is_a, wa, wb)
    base = jnp.where(is_a, 0, wa)
    off9 = jnp.maximum(wa - 9, 0)
    off6 = jnp.maximum(wa - 6, 0)
    offr = jnp.maximum(n0 - 6, 0)

    barrier = pltpu.get_barrier_semaphore()
    for dev in xs + ys + zs + [mate, outer]:
        pl.semaphore_signal(barrier, inc=1, device_id=(dev,), device_id_type=MESH)

    loads = [pltpu.make_async_copy(feat_any, feat, lsem.at[0]), pltpu.make_async_copy(cot_any, cot, lsem.at[1])]
    for load in loads:
        load.start()
    s9, s6 = jnp.where(is_a, off9, 0), jnp.where(is_a, off6, 0)
    h3 = jnp.where(is_a, 0, jnp.maximum(wb - 3, 0))
    sbias[...] = jnp.zeros_like(sbias)
    sbias[0:1, 0:12] = in_bias[...].astype(F32).reshape(1, 12)
    s1[:, C:512] = sbias[...].T[0:16].astype(BF16)
    pad4 = jnp.zeros((4, C), F32)
    s1[:, 0:C] = jnp.concatenate([w_in_t[...].astype(F32), pad4], axis=0).astype(BF16)
    s2[...] = jnp.concatenate([w_out[...].astype(F32), pad4], axis=0).astype(BF16)
    pl.semaphore_wait(barrier, 11)

    first = []
    for o in range(3):
        first.append(send(s1, bx1.at[x], sems, 2 + o, xs[o]))
        first.append(send(s2, bx2.at[x], sems, 5 + o, xs[o]))
    bx1[x] = s1[...]
    bx2[x] = s2[...]
    loads[0].wait()
    for i in range(3):
        hsend[i] = feat[h3 + i]
    xhalo = (xhalo_a, xhalo_b, xhalo_c)
    halo_in = []
    for g in range(3):
        lanes = pl.ds(g * 128, 128)
        halo_in.append(send(hsend.at[:, :, lanes], xhalo[g], sems, (0, 59, 60)[g], outer))
    for i in range(9):
        xsend[i] = feat[s9 + i]
    mate_in = send(xsend, xmate, sems, 1, mate)
    fill_taps(taps, tapb, False)
    fill_taps(taps, tapf, True)
    clear_pads(xf)
    clear_pads(df)
    wait_all(first)
    for ch in range(3):
        rows4 = slice(ch * 4, ch * 4 + 4)
        w1g[core, ch, z, y] = jnp.concatenate([bx1[q].astype(F32)[rows4] for q in range(4)], axis=0).astype(BF16)
        w2g[core, ch, z, y] = jnp.concatenate([bx2[q].astype(F32)[rows4] for q in range(4)], axis=0).astype(BF16)
    second = []
    for o in range(3):
        second.append(send(w1g.at[core, :, z, y], w1g.at[core, :, z, y], sems, 9 + o, ys[o]))
        second.append(send(w2g.at[core, :, z, y], w2g.at[core, :, z, y], sems, 12 + o, zs[o]))
    def pass_on(ch):
        wait_all(third[ch])
        return [send(w1g.at[core, ch], w1g.at[core, ch], sems, 101 + 2 * ch, mate),
                send(w2g.at[core, ch], w2g.at[core, ch], sems, 102 + 2 * ch, mate)]
    mate_in.wait()

    def place_x(g):
        lanes = slice(g * 128, g * 128 + 128)

        def body(i, _):
            p = p0 + i - 3
            q = p - base
            own = feat[jnp.clip(q, 0, CAP - 1), :, lanes].astype(F32)
            other = xmate[jnp.clip(jnp.where(is_a, p - wa, p - off9), 0, 8), :, lanes].astype(F32)
            edge = xhalo[g][jnp.clip(jnp.where(is_a, p + 3, p - pair), 0, 2)].astype(F32)
            is_own = (q >= 0) & (q < mine)
            is_edge = jnp.where(is_a, p < 0, p >= pair)
            gone = (i >= n + 6) | (is_edge & jnp.where(is_a, me == 0, me == N_DEV - 1))
            val = jnp.where(is_own, own, jnp.where(is_edge, edge, other))
            xf[i, g, 8:8 + ROWS, :] = jnp.where(gone, 0.0, val)
            return 0
        lax.fori_loop(0, XC, body, 0)
    halo_in[0].wait()
    place_x(0)
    conv_group(xf, tapb, conv, 0)
    wait_all(second)
    third = []
    for ch in range(3):
        copies = []
        for o in range(3):
            copies.append(send(w1g.at[core, ch, z], w1g.at[core, ch, z], sems, 83 + ch * 6 + o, zs[o]))
            copies.append(send(w2g.at[core, ch, :, y], w2g.at[core, ch, :, y], sems, 83 + ch * 6 + 3 + o, ys[o]))
        third.append(copies)
    loads[1].wait()
    for i in range(6):
        csend[i] = cot[s6 + i]
    cot_in = send(csend, cmate, sems, 8, mate)
    halo_in[1].wait()
    halo_in[2].wait()
    place_x(1)
    conv_group(xf, tapb, conv, 1)
    place_x(2)

    def place_cot(j, _):
        p = p0 + j
        q = p - base
        own = cot[jnp.clip(q, 0, CAP - 1)].astype(F32)
        other = cmate[jnp.clip(jnp.where(is_a, p - wa, p - off6), 0, 5)].astype(F32)
        val = jnp.where((q >= 0) & (q < mine), own, other)
        cotb[j] = jnp.where(j >= n, 0.0, val).astype(BF16)
        return 0
    conv_group(xf, tapb, conv, 2)
    passed = [pass_on(0)]
    cot_in.wait()
    lax.fori_loop(0, NC, place_cot, 0)
    conv[NC - 1] = jnp.zeros((3, ROWS, 128), F32)
    vacc[...] = jnp.zeros_like(vacc)
    vecs = tuple(ref[...].astype(F32).reshape(1, C) for ref in (dw_bias, ln_gain, ln_bias, layer_scale))

    def before(s, _):
        norm_step(s, conv, cotb, vecs, nrm, nrm_t, dm, dm_t, nraw_s, inv_s, vacc)
        return 0
    lax.fori_loop(0, NC // 2, before, 0)

    sums_w = [jnp.zeros((8, C), F32)]
    rs1, rs2 = {}, []

    def weight_grads(ch, own_half, act_s, dpre_s):
        half = core if own_half else 1 - core
        b1 = jnp.dot(nrm_t[...], dpre_s[...], preferred_element_type=F32).T
        b2 = jnp.dot(dm_t[...], act_s[...], preferred_element_type=F32).T
        sums_w[0] += (b2 * w2g[half, ch].reshape(256, C).astype(F32)).reshape(32, 8, C).sum(0)
        to1, to2 = (c1, c2) if own_half else (g1b, g2b)
        to1[ch] = b1.astype(BF16).reshape(4, 4, 16, 512)
        to2[ch] = b2.astype(BF16).reshape(4, 4, 16, C)

    def give(ch):
        rs1[ch] = [send(g1b.at[ch], rc1.at[ch], sems, 125 + 2 * ch, mate),
                   send(g2b.at[ch], rc2.at[ch], sems, 126 + 2 * ch, mate)]

    def join(ch):
        wait_all(rs1[ch])
        for q in range(4):
            c1[ch, q] = (c1[ch, q].astype(F32) + rc1[ch, q].astype(F32)).astype(BF16)
            c2[ch, q] = (c2[ch, q].astype(F32) + rc2[ch, q].astype(F32)).astype(BF16)
        copies = []
        for o in range(3):
            k = 107 + ch * 6 + o
            copies.append(send(c1.at[ch, lax.rem(z + o + 1, 4)], rz1.at[ch, o], sems, k, zs[o]))
            copies.append(send(c2.at[ch, :, lax.rem(y + o + 1, 4)], ry2.at[ch, o], sems, k + 3, ys[o]))
        rs2.append(copies)

    order = [(0, True), (0, False), (1, False), (1, True), (2, False), (2, True)]
    hold = ((act_a, dpre_a), (act_b, dpre_b))
    for turn, (ch, own_half) in enumerate(order):
        half = core if own_half else 1 - core
        if turn in (1, 2):
            passed.append(pass_on(turn))
        if not own_half:
            wait_all(passed[ch])
        mwa[...] = w1g[half, ch].reshape(256, 512).T
        mwb[...] = w2g[half, ch].reshape(256, C).T
        wr[...] = w1g[half, ch].reshape(256, 512)[:, 0:C]
        if turn > 0:
            weight_grads(*order[turn - 1], *hold[(turn - 1) % 2])
        hidden_block(turn == 0, nrm, dm, mwa, mwb, wr, *hold[turn % 2], dn_s)
        if turn > 0 and not order[turn - 1][1]:
            give(order[turn - 1][0])
        if turn in (3, 4):
            join(turn - 3)
    weight_grads(*order[5], *hold[1])
    join(2)
    srow = sums_w[0]
    vacc[3] = srow

    def after(s, _):
        denorm_step(s, dn_s, nraw_s, inv_s, vecs[1], vacc, dcv)
        return 0
    lax.fori_loop(0, NC // 2, after, 0)

    last_at = jnp.maximum(n - 3, 0)
    inner_at, outer_at = jnp.where(is_a, last_at, 0), jnp.where(is_a, 0, last_at)
    for i in range(3):
        dsend[0, i] = dcv[inner_at + i]
        dsend[1, i] = dcv[outer_at + i]
    halo_d = [send(dsend.at[0], dhalo.at[0], sems, 23, mate), send(dsend.at[1], dhalo.at[1], sems, 24, outer)]
    def place_d(j, _):
        put_column(df, j + 3, dcv[j])
        return 0
    lax.fori_loop(0, NC, place_d, 0)
    for g in range(3):
        kernel_grads(xf, df, kacc, g)
    def kout(i, _):
        krow[pl.ds(i, 1), :] = jnp.concatenate([jnp.sum(kacc[i, g], axis=0, keepdims=True) for g in range(3)], axis=1)
        return 0
    lax.fori_loop(0, 49, kout, 0, unroll=7)
    rows = [jnp.sum(vacc[i], axis=0, keepdims=True) for i in range(5)]
    krow[49:56, :] = jnp.zeros((7, C), F32)
    krow[56:64, :] = jnp.concatenate(rows + [jnp.zeros((3, C), F32)], axis=0)
    cur[...] = krow[...].reshape(2, 2, 16, C)

    def sum_send(stage, groups):
        copies = []
        for h, group in enumerate(groups):
            for i, dev in enumerate(group):
                k = stage * 6 + h * 3 + i
                copies.append(send(part_sum.at[stage, h], slots.at[k], sems, 65 + k, dev))
        return copies

    def sum_take(stage, copies):
        wait_all(copies)
        for h in range(2):
            k = stage * 6 + h * 3
            part_sum[stage + 1, h] = part_sum[stage, h] + slots[k] + slots[k + 1] + slots[k + 2]

    first_sum = send(cur.at[1 - core], mslot, sems, 46, mate)
    for copies in rs2:
        wait_all(copies)
    rs3 = []

    def add_second(i, _):
        ch, q = i // 4, lax.rem(i, 4)
        t1[ch, q] = (c1[ch, z, q].astype(F32) + rz1[ch, 0, q].astype(F32) + rz1[ch, 1, q].astype(F32)
                     + rz1[ch, 2, q].astype(F32)).astype(BF16)
        t2[ch, q] = (c2[ch, q, y].astype(F32) + ry2[ch, 0, q].astype(F32) + ry2[ch, 1, q].astype(F32)
                     + ry2[ch, 2, q].astype(F32)).astype(BF16)
        return 0
    lax.fori_loop(0, 12, add_second, 0)
    for o in range(3):
        rs3.append(send(t1.at[:, lax.rem(y + o + 1, 4)], ry1.at[o], sems, 33 + o, ys[o]))
        rs3.append(send(t2.at[:, lax.rem(z + o + 1, 4)], rz2.at[o], sems, 36 + o, zs[o]))
    first_sum.wait()
    for h in range(2):
        part_sum[0, h] = cur[core, h] + mslot[h]
    sums = sum_send(0, (ys, zs))
    wait_all(halo_d)

    def place_edges(i, _):
        k = jnp.clip(i - n - 3, 0, 2)
        left = jnp.where(is_a, dhalo[1, jnp.clip(i, 0, 2)].astype(F32), dhalo[0, jnp.clip(i, 0, 2)].astype(F32))
        right = jnp.where(is_a, dhalo[0, k].astype(F32), dhalo[1, k].astype(F32))
        left = jnp.where(me == 0, 0.0, left)
        right = jnp.where((i >= n + 6) | (me == N_DEV - 1), 0.0, right)
        own = dcv[jnp.clip(i - 3, 0, NC - 1)].astype(F32)
        put_column(df, i, jnp.where(i < 3, left, jnp.where(i < n + 3, own, right)))
        return 0
    lax.fori_loop(0, XC, place_edges, 0)
    back_group(df, tapf, cotb, dimg, 0)
    sum_take(0, sums)
    sums = sum_send(1, (zs, xs))
    wait_all(rs3)
    for ch in range(3):
        u1 = (t1[ch, y].astype(F32) + ry1[0, ch].astype(F32)) + (ry1[1, ch].astype(F32) + ry1[2, ch].astype(F32))
        u2 = (t2[ch, z].astype(F32) + rz2[0, ch].astype(F32)) + (rz2[1, ch].astype(F32) + rz2[2, ch].astype(F32))
        for q in range(4):
            p1[q, ch * 4:ch * 4 + 4, :] = u1[q * 4:q * 4 + 4]
            p2[q, ch * 4:ch * 4 + 4, :] = u2[q * 4:q * 4 + 4]
    for q in range(4):
        p1[q, 12:16, :] = jnp.zeros((4, 512), F32)
        p2[q, 12:16, :] = jnp.zeros((4, C), F32)
    rs4 = []
    for o in range(3):
        q = lax.rem(x + o + 1, 4)
        rs4.append(send(p1.at[q], rx1.at[o], sems, 39 + o, xs[o]))
        rs4.append(send(p2.at[q], rx2.at[o], sems, 42 + o, xs[o]))
    back_group(df, tapf, cotb, dimg, 1)
    sum_take(1, sums)
    sums = sum_send(2, (xs, ys))
    back_group(df, tapf, cotb, dimg, 2)
    sr = jnp.where(is_a, offr, 0)
    for i in range(6):
        rsend[i] = dimg[sr + i]
    back = send(rsend, rmate, sems, 45, mate)
    wait_all(rs4)
    o1_out[...] = (p1[x] + rx1[0] + rx1[1] + rx1[2]) * SCALE
    o2_out[...] = (p2[x] + rx2[0] + rx2[1] + rx2[2]) * SCALE
    sum_take(2, sums)
    total[core] = part_sum[3]
    last = send(total.at[core], total.at[core], sems, 47, mate)
    dimg_out[...] = dimg[...]
    last.wait()
    small_out[...] = total[...].reshape(64, C) * SCALE
    back.wait()
    rmate_out[...] = rmate[...]


def finish_kernel(widths, place, dimg, rmate, total, o1, o2, out_bias, layer_scale,
                  d_out, g_kernel, g_bias, g_gain, g_lbias, g_win, g_ibias, g_wout, g_obias, g_scale):
    me = place[0]
    core = lax.rem(me, 2)
    is_a = core == 0
    wa, wb = widths[me - core], widths[me - core + 1]
    n0 = (wa + wb + 1) // 2
    p0 = jnp.where(is_a, 0, n0)
    mine = jnp.where(is_a, wa, wb)
    base = jnp.where(is_a, 0, wa)
    offr = jnp.maximum(n0 - 6, 0)

    def place_out(s, _):
        p = base + s
        own = dimg[jnp.clip(p - p0, 0, NC - 1)]
        other = rmate[jnp.clip(jnp.where(is_a, p - n0, p - offr), 0, 5)]
        is_own = jnp.where(is_a, p < n0, p >= n0)
        val = jnp.where(is_own, own.astype(F32), other.astype(F32))
        d_out[s] = jnp.where(s >= mine, 0.0, val).astype(BF16)
        return 0
    lax.fori_loop(0, CAP, place_out, 0)
    g_kernel[...] = total[0:49]

    def row(i):
        return total[i:i + 1, :]
    g_gain[...] = row(56).reshape(C)
    g_lbias[...] = row(57).reshape(C)
    g_obias[...] = row(58).reshape(C)
    g_bias[...] = row(60).reshape(C)
    ls, ob = layer_scale[...].astype(F32).reshape(1, C), out_bias[...].astype(F32).reshape(1, C)
    g_scale[...] = ((row(59) + ob * row(58)) / ls).reshape(C)
    g_win[...] = o1[0:12, 0:C]
    g_ibias[...] = o1[:, C:512].T[0:1, 0:12].reshape(12)
    g_wout[...] = o2[0:12]


def finish(widths, place, *args):
    def f(*shape, dtype=F32):
        return jax.ShapeDtypeStruct(shape, dtype)
    return pl.pallas_call(
        finish_kernel,
        out_shape=(f(CAP, ROWS, C, dtype=BF16), f(49, C), f(C), f(C), f(C), f(12, C), f(12), f(12, C), f(C), f(C)),
        in_specs=[SMEM] * 2 + [VMEM] * 7,
        out_specs=[VMEM] * 10,
        compiler_params=pltpu.CompilerParams(vmem_limit_bytes=60 * 2**20),
        name="place_results",
    )(widths, place, *args)


def fused(*args):
    def v(*shape, dtype=BF16):
        return pltpu.VMEM(shape, dtype)
    return pl.pallas_call(
        kernel,
        out_shape=(
            jax.ShapeDtypeStruct((NC, ROWS, C), BF16),
            jax.ShapeDtypeStruct((6, ROWS, C), BF16),
            jax.ShapeDtypeStruct((64, C), F32),
            jax.ShapeDtypeStruct((16, 512), F32),
            jax.ShapeDtypeStruct((16, C), F32),
        ),
        in_specs=[SMEM] + [pl.BlockSpec(memory_space=pl.ANY)] * 2 + [VMEM] * 8,
        out_specs=[VMEM] * 5,
        scratch_shapes=[
            v(CAP, ROWS, C), v(CAP, ROWS, C), v(16, 512), v(16, C), v(128, 128, dtype=F32),
            v(9, ROWS, C), v(9, ROWS, C), v(3, ROWS, C), v(3, ROWS, 128), v(3, ROWS, 128), v(3, ROWS, 128), v(6, ROWS, C), v(6, ROWS, C),
            v(4, 16, 512), v(4, 16, C), v(2, 3, 4, 4, 16, 512), v(2, 3, 4, 4, 16, C),
            v(XC, 3, RP, 128, dtype=F32), v(XC, 3, RP, 128, dtype=F32),
            v(49, 3, 8, 128, dtype=F32), v(49, 3, 8, 128, dtype=F32),
            v(NC, 3, ROWS, 128, dtype=F32), v(NC, ROWS, C),
            v(TOK, 512), v(512, TOK), v(TOK, C), v(C, TOK), v(TOK, C, dtype=F32), v(TOK, 128, dtype=F32), v(TOK, C, dtype=F32),
            v(TOK, 256), v(TOK, 256), v(TOK, 256), v(TOK, 256), v(512, 256), v(C, 256), v(256, C),
            v(8, 8, C, dtype=F32), v(NC, ROWS, C),
            v(3, 4, 4, 16, 512), v(3, 4, 4, 16, C), v(2, 3, ROWS, C), v(2, 3, ROWS, C),
            v(3, 4, 4, 16, 512), v(3, 4, 4, 16, C), v(3, 4, 4, 16, 512), v(3, 4, 4, 16, C),
            v(3, 3, 4, 16, 512), v(3, 3, 4, 16, C), v(3, 4, 16, 512), v(3, 4, 16, C), v(3, 3, 16, 512), v(3, 3, 16, C),
            v(4, 16, 512, dtype=F32), v(4, 16, C, dtype=F32), v(3, 16, 512, dtype=F32), v(3, 16, C, dtype=F32),
            v(49, 3, 8, 128, dtype=F32), v(64, C, dtype=F32), v(2, 2, 16, C, dtype=F32), v(2, 16, C, dtype=F32),
            v(4, 2, 16, C, dtype=F32), v(18, 16, C, dtype=F32), v(2, 2, 16, C, dtype=F32),
            v(NC, ROWS, C), v(6, ROWS, C), v(6, ROWS, C),
            pltpu.SemaphoreType.DMA((131,)), pltpu.SemaphoreType.DMA((131,)), pltpu.SemaphoreType.DMA((2,)),
        ],
        compiler_params=pltpu.CompilerParams(collective_id=0, has_side_effects=True, vmem_limit_bytes=60 * 2**20),
        name="block_back",
    )(*args)


def local(features, grad_out, widths, dw_kernel, dw_bias, ln_gain, ln_bias,
          w_in, in_bias, w_out, out_bias, layer_scale):
    feat, cot = jnp.transpose(features, (1, 0, 2)), jnp.transpose(grad_out, (1, 0, 2))
    place = lax.axis_index("strip").reshape(1)
    dimg, rmate, total, o1, o2 = fused(widths, feat, cot, w_in.T, in_bias, w_out, dw_kernel,
                                       dw_bias, ln_gain, ln_bias, layer_scale)
    outs = finish(widths, place, dimg, rmate, total, o1, o2, out_bias, layer_scale)
    return (jnp.transpose(outs[0], (1, 0, 2)),) + tuple(outs[1:5]) + (outs[5].T,) + tuple(outs[6:])


def solution(mesh):
    wide = P(None, "strip", None)
    return jax.shard_map(
        local, mesh=mesh,
        in_specs=(wide, wide, P(), P(), P(), P(), P(), P(None, "strip"), P("strip"), P("strip", None), P(), P()),
        out_specs=(wide, P(), P(), P(), P(), P(None, "strip"), P("strip"), P("strip", None), P(), P()),
        check_vma=False)
```

```python
import math

import jax
import jax.numpy as jnp
from jax import lax
from jax.sharding import PartitionSpec as P
from jax.experimental import pallas as pl
from jax.experimental.pallas import tpu as pltpu

ROWS, C, FF, CAP = 128, 384, 1536, 15
N_DEV = 128
NC = 12
NW = 11
XC = NC + 6
RP = ROWS + 16
T = 2 * ROWS
TOK = NC * ROWS
F32, BF16 = jnp.float32, jnp.bfloat16
VMEM = pl.BlockSpec(memory_space=pltpu.VMEM)
SMEM = pl.BlockSpec(memory_space=pltpu.SMEM)
MESH = pl.DeviceIdType.MESH
SCALE = 1.0 / math.sqrt(ROWS * N_DEV * 5)


def gelu_parts(x):
    e = jnp.exp(x * x * -0.5)
    t = 1.0 / (1.0 + (0.3275911 * 0.7071067811865476) * jnp.abs(x))
    q = ((((0.5 * 1.061405429) * t - 0.5 * 1.453152027) * t + 0.5 * 1.421413741) * t - 0.5 * 0.284496736) * t + 0.5 * 0.254829592
    h = q * t * e
    cdf = jnp.where(x >= 0, 1.0 - h, h)
    slope = cdf + x * e * 0.3989422804014327
    return x * cdf, slope


def fill_taps(taps_ref, tapb, flip):
    for g in range(3):
        block = taps_ref[:, g * 128:(g + 1) * 128].astype(F32)
        for i in range(49):
            src = 48 - i if flip else i
            tapb[i, g] = jnp.broadcast_to(block[src:src + 1], (8, 128))


def put_column(xf, dst, block):
    block = block.astype(F32)
    for g in range(3):
        xf[dst, g, 8:8 + ROWS, :] = block[:, g * 128:(g + 1) * 128]


def clear_pads(xf):
    zero = jnp.zeros((8, 128), F32)

    def body(i, _):
        for g in range(3):
            xf[i, g, 0:8, :] = zero
            xf[i, g, RP - 8:RP, :] = zero
        return 0
    lax.fori_loop(0, XC, body, 0)


def conv_rows(xf, tapb, g, r0):
    def aloop(a, accs):
        accs = [list(part_) for part_ in accs]
        ts = [tapb[a * 7 + b, g] for b in range(7)]
        for i in range(NW + 6):
            for k in range(2):
                xv = xf[i, g, pl.ds(r0 + 8 * k + 5 + a, 8), :]
                for b in range(7):
                    if 0 <= i - b < NW:
                        accs[k][i - b] = accs[k][i - b] + ts[b] * xv
        return tuple(tuple(part_) for part_ in accs)
    zero = jnp.zeros((8, 128), F32)
    return lax.fori_loop(0, 7, aloop, ((zero,) * NW,) * 2)


def conv_group(xf, tapb, conv, g):
    def rloop(r, _):
        r0 = pl.multiple_of(r * 16, 16)
        lo, hi = conv_rows(xf, tapb, g, r0)
        for j in range(NW):
            conv[j, g, pl.ds(r0, 16), :] = jnp.concatenate([lo[j], hi[j]], axis=0)
        return 0
    lax.fori_loop(0, 8, rloop, 0)


def back_group(df, tapb, cotb, dimg, g):
    ls = slice(g * 128, g * 128 + 128)

    def rloop(r, _):
        r0 = pl.multiple_of(r * 16, 16)
        lo, hi = conv_rows(df, tapb, g, r0)
        for j in range(NW):
            acc = jnp.concatenate([lo[j], hi[j]], axis=0) + cotb[j, pl.ds(r0, 16), ls].astype(F32)
            dimg[j, pl.ds(r0, 16), ls] = acc.astype(BF16)
        return 0
    lax.fori_loop(0, 8, rloop, 0)


def kernel_grads(xf, df, kacc, g):
    def aloop(a, _):
        def rloop(r, accs):
            r0 = r * 8
            accs = list(accs)
            ds = [df[3 + j, g, pl.ds(pl.multiple_of(r0 + 8, 8), 8), :] for j in range(NW)]
            for i in range(NW + 6):
                xv = xf[i, g, pl.ds(r0 + 5 + a, 8), :]
                for b in range(7):
                    if 0 <= i - b < NW:
                        accs[b] = accs[b] + ds[i - b] * xv
            return tuple(accs)
        accs = lax.fori_loop(0, 16, rloop, tuple(jnp.zeros((8, 128), F32) for _ in range(7)), unroll=8)
        for b in range(7):
            kacc[a * 7 + b, g] = accs[b]
        return 0
    lax.fori_loop(0, 7, aloop, 0)


def part(x):
    return x.reshape(T // 8, 8, C).sum(0)


def norm_step(s, conv, cotb, vecs, nrm, nrm_t, dm, dm_t, nraw_s, inv_s, vacc):
    bias, gain, lbias, ls = vecs
    at = pl.ds(pl.multiple_of(s * T, T), T)
    one_col = (lax.broadcasted_iota(jnp.int32, (T, 128), 1) == 0).astype(BF16)
    v = jnp.concatenate([conv[pl.ds(2 * s, 2), g].reshape(T, 128) for g in range(3)], axis=1) + bias
    v = v.astype(BF16).astype(F32)
    mean = jnp.sum(v, axis=1, keepdims=True) * (1.0 / C)
    cen = v - mean
    inv = lax.rsqrt(jnp.sum(cen * cen, axis=1, keepdims=True) * (1.0 / C) + 1e-6)
    nraw = cen * inv
    normed = jnp.concatenate([(nraw * gain + lbias).astype(BF16), one_col], axis=1)
    dmlp = (cotb[pl.ds(2 * s, 2)].reshape(T, C).astype(F32) * ls).astype(BF16)
    vacc[2] += part(dmlp.astype(F32))
    nrm[at, :] = normed
    nrm_t[:, at] = normed.T
    dm[at, :] = dmlp
    dm_t[:, at] = dmlp.T
    nraw_s[at, :] = nraw
    inv_s[at, :] = jnp.broadcast_to(inv, (T, 128))


def hidden_block(first, nrm, dm, wa, wb, wrows, act_s, dpre_s, dn_s):
    ats = [slice(k * T, k * T + T) for k in range(TOK // T)]

    def front(at):
        return (jnp.dot(nrm[at, :], wa[...], preferred_element_type=F32),
                jnp.dot(dm[at, :], wb[...], preferred_element_type=F32))
    ahead = front(ats[0])
    for i, at in enumerate(ats):
        pre, dact = ahead
        if i + 1 < len(ats):
            ahead = front(ats[i + 1])
        act, slope = gelu_parts(pre)
        act_s[at, :] = act.astype(BF16)
        dpre = (dact * slope).astype(BF16)
        dpre_s[at, :] = dpre
        dn = jnp.dot(dpre, wrows[...], preferred_element_type=F32)
        dn_s[at, :] = dn if first else dn_s[at, :] + dn


def denorm_step(s, dn_s, nraw_s, inv_s, gain, vacc, dcv):
    at = pl.ds(pl.multiple_of(s * T, T), T)
    dn, nraw, inv = dn_s[at, :], nraw_s[at, :], inv_s[at, 0:1]
    vacc[0] += part(dn * nraw)
    vacc[1] += part(dn)
    sc = dn * gain
    m1 = jnp.sum(sc, axis=1, keepdims=True) * (1.0 / C)
    m2 = jnp.sum(sc * nraw, axis=1, keepdims=True) * (1.0 / C)
    dc = (inv * (sc - m1 - nraw * m2)).astype(BF16)
    vacc[4] += part(dc.astype(F32))
    dcv[pl.ds(2 * s, 2)] = dc.reshape(2, ROWS, C)


def peers_of(me, coord, stride):
    return [me + (lax.rem(coord + o, 4) - coord) * stride for o in (1, 2, 3)]


def send(src, dst, sems, idx, dev):
    copy = pltpu.make_async_remote_copy(
        src_ref=src, dst_ref=dst, send_sem=sems[0].at[idx], recv_sem=sems[1].at[idx],
        device_id=(dev,), device_id_type=MESH)
    copy.start()
    return copy


def wait_all(copies):
    for copy in copies:
        copy.wait()


def kernel(widths, feat_any, cot_any, w_in_t, in_bias, w_out, taps, dw_bias, ln_gain, ln_bias, layer_scale,
           dimg_out, rmate_out, small_out, o1_out, o2_out,
           feat, cot, s1, s2, sbias,
           xsend, xmate, hsend, xhalo_a, xhalo_b, xhalo_c, csend, cmate,
           bx1, bx2, w1g, w2g, xf, df, tapb, tapf, conv, cotb, nrm, nrm_t, dm, dm_t, nraw_s, inv_s, dn_s,
           act_a, dpre_a, act_b, dpre_b, mwa, mwb, wr, vacc, dcv,
           g1b, g2b, dsend, dhalo, rc1, rc2, c1, c2, rz1, ry2, t1, t2, ry1, rz2, p1, p2, rx1, rx2,
           kacc, krow, cur, mslot, part_sum, slots, total, dimg, rsend, rmate, ssem, rsem, lsem):
    me = lax.axis_index("strip")
    core = lax.rem(me, 2)
    y = lax.rem(me // 2, 4)
    x = lax.rem(me // 8, 4)
    z = me // 32
    xs, ys, zs = peers_of(me, x, 8), peers_of(me, y, 2), peers_of(me, z, 32)
    mate = me + 1 - 2 * core
    outer = lax.rem(me + 2 * core - 1 + N_DEV, N_DEV)
    sems = (ssem, rsem)
    is_a = core == 0
    wa, wb = widths[me - core], widths[me - core + 1]
    pair = wa + wb
    n0 = (pair + 1) // 2
    n = jnp.where(is_a, n0, pair - n0)
    p0 = jnp.where(is_a, 0, n0)
    mine = jnp.where(is_a, wa, wb)
    base = jnp.where(is_a, 0, wa)
    off9 = jnp.maximum(wa - 9, 0)
    off6 = jnp.maximum(wa - 6, 0)
    offr = jnp.maximum(n0 - 6, 0)

    barrier = pltpu.get_barrier_semaphore()
    for dev in xs + ys + zs + [mate, outer]:
        pl.semaphore_signal(barrier, inc=1, device_id=(dev,), device_id_type=MESH)

    loads = [pltpu.make_async_copy(feat_any, feat, lsem.at[0]), pltpu.make_async_copy(cot_any, cot, lsem.at[1])]
    for load in loads:
        load.start()
    s9, s6 = jnp.where(is_a, off9, 0), jnp.where(is_a, off6, 0)
    h3 = jnp.where(is_a, 0, jnp.maximum(wb - 3, 0))
    sbias[...] = jnp.zeros_like(sbias)
    sbias[0:1, 0:12] = in_bias[...].astype(F32).reshape(1, 12)
    s1[:, C:512] = sbias[...].T[0:16].astype(BF16)
    pad4 = jnp.zeros((4, C), F32)
    s1[:, 0:C] = jnp.concatenate([w_in_t[...].astype(F32), pad4], axis=0).astype(BF16)
    s2[...] = jnp.concatenate([w_out[...].astype(F32), pad4], axis=0).astype(BF16)
    pl.semaphore_wait(barrier, 11)

    first = []
    for o in range(3):
        first.append(send(s1, bx1.at[x], sems, 2 + o, xs[o]))
        first.append(send(s2, bx2.at[x], sems, 5 + o, xs[o]))
    bx1[x] = s1[...]
    bx2[x] = s2[...]
    loads[0].wait()
    for i in range(3):
        hsend[i] = feat[h3 + i]
    xhalo = (xhalo_a, xhalo_b, xhalo_c)
    halo_in = []
    for g in range(3):
        lanes = pl.ds(g * 128, 128)
        halo_in.append(send(hsend.at[:, :, lanes], xhalo[g], sems, (0, 59, 60)[g], outer))
    for i in range(9):
        xsend[i] = feat[s9 + i]
    mate_in = send(xsend, xmate, sems, 1, mate)
    fill_taps(taps, tapb, False)
    fill_taps(taps, tapf, True)
    clear_pads(xf)
    clear_pads(df)
    wait_all(first)
    for ch in range(3):
        rows4 = slice(ch * 4, ch * 4 + 4)
        w1g[core, ch, z, y] = jnp.concatenate([bx1[q].astype(F32)[rows4] for q in range(4)], axis=0).astype(BF16)
        w2g[core, ch, z, y] = jnp.concatenate([bx2[q].astype(F32)[rows4] for q in range(4)], axis=0).astype(BF16)
    second = []
    for o in range(3):
        second.append(send(w1g.at[core, :, z, y], w1g.at[core, :, z, y], sems, 9 + o, ys[o]))
        second.append(send(w2g.at[core, :, z, y], w2g.at[core, :, z, y], sems, 12 + o, zs[o]))
    def pass_on(ch):
        wait_all(third[ch])
        return [send(w1g.at[core, ch], w1g.at[core, ch], sems, 101 + 2 * ch, mate),
                send(w2g.at[core, ch], w2g.at[core, ch], sems, 102 + 2 * ch, mate)]
    mate_in.wait()

    def place_x(g):
        lanes = slice(g * 128, g * 128 + 128)

        def body(i, _):
            p = p0 + i - 3
            q = p - base
            own = feat[jnp.clip(q, 0, CAP - 1), :, lanes].astype(F32)
            other = xmate[jnp.clip(jnp.where(is_a, p - wa, p - off9), 0, 8), :, lanes].astype(F32)
            edge = xhalo[g][jnp.clip(jnp.where(is_a, p + 3, p - pair), 0, 2)].astype(F32)
            is_own = (q >= 0) & (q < mine)
            is_edge = jnp.where(is_a, p < 0, p >= pair)
            gone = (i >= n + 6) | (is_edge & jnp.where(is_a, me == 0, me == N_DEV - 1))
            val = jnp.where(is_own, own, jnp.where(is_edge, edge, other))
            xf[i, g, 8:8 + ROWS, :] = jnp.where(gone, 0.0, val)
            return 0
        lax.fori_loop(0, XC, body, 0)
    halo_in[0].wait()
    place_x(0)
    conv_group(xf, tapb, conv, 0)
    wait_all(second)
    third = []
    for ch in range(3):
        copies = []
        for o in range(3):
            copies.append(send(w1g.at[core, ch, z], w1g.at[core, ch, z], sems, 83 + ch * 6 + o, zs[o]))
            copies.append(send(w2g.at[core, ch, :, y], w2g.at[core, ch, :, y], sems, 83 + ch * 6 + 3 + o, ys[o]))
        third.append(copies)
    loads[1].wait()
    for i in range(6):
        csend[i] = cot[s6 + i]
    cot_in = send(csend, cmate, sems, 8, mate)
    halo_in[1].wait()
    halo_in[2].wait()
    place_x(1)
    conv_group(xf, tapb, conv, 1)
    place_x(2)

    def place_cot(j, _):
        p = p0 + j
        q = p - base
        own = cot[jnp.clip(q, 0, CAP - 1)].astype(F32)
        other = cmate[jnp.clip(jnp.where(is_a, p - wa, p - off6), 0, 5)].astype(F32)
        val = jnp.where((q >= 0) & (q < mine), own, other)
        cotb[j] = jnp.where(j >= n, 0.0, val).astype(BF16)
        return 0
    conv_group(xf, tapb, conv, 2)
    passed = [pass_on(0)]
    cot_in.wait()
    lax.fori_loop(0, NC, place_cot, 0)
    conv[NC - 1] = jnp.zeros((3, ROWS, 128), F32)
    vacc[...] = jnp.zeros_like(vacc)
    vecs = tuple(ref[...].astype(F32).reshape(1, C) for ref in (dw_bias, ln_gain, ln_bias, layer_scale))

    def before(s, _):
        norm_step(s, conv, cotb, vecs, nrm, nrm_t, dm, dm_t, nraw_s, inv_s, vacc)
        return 0
    lax.fori_loop(0, NC // 2, before, 0, unroll=2)

    sums_w = [jnp.zeros((8, C), F32)]
    rs1, rs2 = {}, []

    def weight_grads(ch, own_half, act_s, dpre_s):
        half = core if own_half else 1 - core
        b1 = jnp.dot(nrm_t[...], dpre_s[...], preferred_element_type=F32).T
        b2 = jnp.dot(dm_t[...], act_s[...], preferred_element_type=F32).T
        sums_w[0] += (b2 * w2g[half, ch].reshape(256, C).astype(F32)).reshape(32, 8, C).sum(0)
        to1, to2 = (c1, c2) if own_half else (g1b, g2b)
        to1[ch] = b1.astype(BF16).reshape(4, 4, 16, 512)
        to2[ch] = b2.astype(BF16).reshape(4, 4, 16, C)

    def give(ch):
        rs1[ch] = [send(g1b.at[ch], rc1.at[ch], sems, 125 + 2 * ch, mate),
                   send(g2b.at[ch], rc2.at[ch], sems, 126 + 2 * ch, mate)]

    def join(ch):
        wait_all(rs1[ch])
        for q in range(4):
            c1[ch, q] = (c1[ch, q].astype(F32) + rc1[ch, q].astype(F32)).astype(BF16)
            c2[ch, q] = (c2[ch, q].astype(F32) + rc2[ch, q].astype(F32)).astype(BF16)
        copies = []
        for o in range(3):
            k = 107 + ch * 6 + o
            copies.append(send(c1.at[ch, lax.rem(z + o + 1, 4)], rz1.at[ch, o], sems, k, zs[o]))
            copies.append(send(c2.at[ch, :, lax.rem(y + o + 1, 4)], ry2.at[ch, o], sems, k + 3, ys[o]))
        rs2.append(copies)

    order = [(0, True), (0, False), (1, False), (1, True), (2, False), (2, True)]
    hold = ((act_a, dpre_a), (act_b, dpre_b))
    for turn, (ch, own_half) in enumerate(order):
        half = core if own_half else 1 - core
        if turn in (1, 2):
            passed.append(pass_on(turn))
        if not own_half:
            wait_all(passed[ch])
        mwa[...] = w1g[half, ch].reshape(256, 512).T
        mwb[...] = w2g[half, ch].reshape(256, C).T
        wr[...] = w1g[half, ch].reshape(256, 512)[:, 0:C]
        if turn > 0:
            weight_grads(*order[turn - 1], *hold[(turn - 1) % 2])
        hidden_block(turn == 0, nrm, dm, mwa, mwb, wr, *hold[turn % 2], dn_s)
        if turn > 0 and not order[turn - 1][1]:
            give(order[turn - 1][0])
        if turn in (3, 4):
            join(turn - 3)
    weight_grads(*order[5], *hold[1])
    join(2)
    srow = sums_w[0]
    vacc[3] = srow

    def after(s, _):
        denorm_step(s, dn_s, nraw_s, inv_s, vecs[1], vacc, dcv)
        return 0
    lax.fori_loop(0, NC // 2, after, 0, unroll=2)

    last_at = jnp.maximum(n - 3, 0)
    inner_at, outer_at = jnp.where(is_a, last_at, 0), jnp.where(is_a, 0, last_at)
    for i in range(3):
        dsend[0, i] = dcv[inner_at + i]
        dsend[1, i] = dcv[outer_at + i]
    halo_d = [send(dsend.at[0], dhalo.at[0], sems, 23, mate), send(dsend.at[1], dhalo.at[1], sems, 24, outer)]
    def place_d(j, _):
        put_column(df, j + 3, dcv[j])
        return 0
    lax.fori_loop(0, NC, place_d, 0)
    for g in range(3):
        kernel_grads(xf, df, kacc, g)
    def kout(i, _):
        krow[pl.ds(i, 1), :] = jnp.concatenate([jnp.sum(kacc[i, g], axis=0, keepdims=True) for g in range(3)], axis=1)
        return 0
    lax.fori_loop(0, 49, kout, 0, unroll=7)
    rows = [jnp.sum(vacc[i], axis=0, keepdims=True) for i in range(5)]
    krow[49:56, :] = jnp.zeros((7, C), F32)
    krow[56:64, :] = jnp.concatenate(rows + [jnp.zeros((3, C), F32)], axis=0)
    cur[...] = krow[...].reshape(2, 2, 16, C)

    def sum_send(stage, groups):
        copies = []
        for h, group in enumerate(groups):
            for i, dev in enumerate(group):
                k = stage * 6 + h * 3 + i
                copies.append(send(part_sum.at[stage, h], slots.at[k], sems, 65 + k, dev))
        return copies

    def sum_take(stage, copies):
        wait_all(copies)
        for h in range(2):
            k = stage * 6 + h * 3
            part_sum[stage + 1, h] = part_sum[stage, h] + slots[k] + slots[k + 1] + slots[k + 2]

    first_sum = send(cur.at[1 - core], mslot, sems, 46, mate)
    for copies in rs2:
        wait_all(copies)
    rs3 = []

    def add_second(i, _):
        ch, q = i // 4, lax.rem(i, 4)
        t1[ch, q] = (c1[ch, z, q].astype(F32) + rz1[ch, 0, q].astype(F32) + rz1[ch, 1, q].astype(F32)
                     + rz1[ch, 2, q].astype(F32)).astype(BF16)
        t2[ch, q] = (c2[ch, q, y].astype(F32) + ry2[ch, 0, q].astype(F32) + ry2[ch, 1, q].astype(F32)
                     + ry2[ch, 2, q].astype(F32)).astype(BF16)
        return 0
    lax.fori_loop(0, 12, add_second, 0)
    for o in range(3):
        rs3.append(send(t1.at[:, lax.rem(y + o + 1, 4)], ry1.at[o], sems, 33 + o, ys[o]))
        rs3.append(send(t2.at[:, lax.rem(z + o + 1, 4)], rz2.at[o], sems, 36 + o, zs[o]))
    first_sum.wait()
    for h in range(2):
        part_sum[0, h] = cur[core, h] + mslot[h]
    sums = sum_send(0, (ys, zs))
    wait_all(halo_d)

    def place_edges(i, _):
        k = jnp.clip(i - n - 3, 0, 2)
        left = jnp.where(is_a, dhalo[1, jnp.clip(i, 0, 2)].astype(F32), dhalo[0, jnp.clip(i, 0, 2)].astype(F32))
        right = jnp.where(is_a, dhalo[0, k].astype(F32), dhalo[1, k].astype(F32))
        left = jnp.where(me == 0, 0.0, left)
        right = jnp.where((i >= n + 6) | (me == N_DEV - 1), 0.0, right)
        own = dcv[jnp.clip(i - 3, 0, NC - 1)].astype(F32)
        put_column(df, i, jnp.where(i < 3, left, jnp.where(i < n + 3, own, right)))
        return 0
    lax.fori_loop(0, XC, place_edges, 0)
    back_group(df, tapf, cotb, dimg, 0)
    sum_take(0, sums)
    sums = sum_send(1, (zs, xs))
    wait_all(rs3)
    for ch in range(3):
        u1 = (t1[ch, y].astype(F32) + ry1[0, ch].astype(F32)) + (ry1[1, ch].astype(F32) + ry1[2, ch].astype(F32))
        u2 = (t2[ch, z].astype(F32) + rz2[0, ch].astype(F32)) + (rz2[1, ch].astype(F32) + rz2[2, ch].astype(F32))
        for q in range(4):
            p1[q, ch * 4:ch * 4 + 4, :] = u1[q * 4:q * 4 + 4]
            p2[q, ch * 4:ch * 4 + 4, :] = u2[q * 4:q * 4 + 4]
    for q in range(4):
        p1[q, 12:16, :] = jnp.zeros((4, 512), F32)
        p2[q, 12:16, :] = jnp.zeros((4, C), F32)
    rs4 = []
    for o in range(3):
        q = lax.rem(x + o + 1, 4)
        rs4.append(send(p1.at[q], rx1.at[o], sems, 39 + o, xs[o]))
        rs4.append(send(p2.at[q], rx2.at[o], sems, 42 + o, xs[o]))
    back_group(df, tapf, cotb, dimg, 1)
    sum_take(1, sums)
    sums = sum_send(2, (xs, ys))
    back_group(df, tapf, cotb, dimg, 2)
    sr = jnp.where(is_a, offr, 0)
    for i in range(6):
        rsend[i] = dimg[sr + i]
    back = send(rsend, rmate, sems, 45, mate)
    wait_all(rs4)
    o1_out[...] = (p1[x] + rx1[0] + rx1[1] + rx1[2]) * SCALE
    o2_out[...] = (p2[x] + rx2[0] + rx2[1] + rx2[2]) * SCALE
    sum_take(2, sums)
    total[core] = part_sum[3]
    last = send(total.at[core], total.at[core], sems, 47, mate)
    dimg_out[...] = dimg[...]
    last.wait()
    small_out[...] = total[...].reshape(64, C) * SCALE
    back.wait()
    rmate_out[...] = rmate[...]


def finish_kernel(widths, place, dimg, rmate, total, o1, o2, out_bias, layer_scale,
                  d_out, g_kernel, g_bias, g_gain, g_lbias, g_win, g_ibias, g_wout, g_obias, g_scale):
    me = place[0]
    core = lax.rem(me, 2)
    is_a = core == 0
    wa, wb = widths[me - core], widths[me - core + 1]
    n0 = (wa + wb + 1) // 2
    p0 = jnp.where(is_a, 0, n0)
    mine = jnp.where(is_a, wa, wb)
    base = jnp.where(is_a, 0, wa)
    offr = jnp.maximum(n0 - 6, 0)

    def place_out(s, _):
        p = base + s
        own = dimg[jnp.clip(p - p0, 0, NC - 1)]
        other = rmate[jnp.clip(jnp.where(is_a, p - n0, p - offr), 0, 5)]
        is_own = jnp.where(is_a, p < n0, p >= n0)
        val = jnp.where(is_own, own.astype(F32), other.astype(F32))
        d_out[s] = jnp.where(s >= mine, 0.0, val).astype(BF16)
        return 0
    lax.fori_loop(0, CAP, place_out, 0, unroll=3)
    g_kernel[...] = total[0:49]

    def row(i):
        return total[i:i + 1, :]
    g_gain[...] = row(56).reshape(C)
    g_lbias[...] = row(57).reshape(C)
    g_obias[...] = row(58).reshape(C)
    g_bias[...] = row(60).reshape(C)
    ls, ob = layer_scale[...].astype(F32).reshape(1, C), out_bias[...].astype(F32).reshape(1, C)
    g_scale[...] = ((row(59) + ob * row(58)) / ls).reshape(C)
    g_win[...] = o1[0:12, 0:C]
    g_ibias[...] = o1[:, C:512].T[0:1, 0:12].reshape(12)
    g_wout[...] = o2[0:12]


def finish(widths, place, *args):
    def f(*shape, dtype=F32):
        return jax.ShapeDtypeStruct(shape, dtype)
    return pl.pallas_call(
        finish_kernel,
        out_shape=(f(CAP, ROWS, C, dtype=BF16), f(49, C), f(C), f(C), f(C), f(12, C), f(12), f(12, C), f(C), f(C)),
        in_specs=[SMEM] * 2 + [VMEM] * 7,
        out_specs=[VMEM] * 10,
        compiler_params=pltpu.CompilerParams(vmem_limit_bytes=60 * 2**20),
        name="place_results",
    )(widths, place, *args)


def fused(*args):
    def v(*shape, dtype=BF16):
        return pltpu.VMEM(shape, dtype)
    return pl.pallas_call(
        kernel,
        out_shape=(
            jax.ShapeDtypeStruct((NC, ROWS, C), BF16),
            jax.ShapeDtypeStruct((6, ROWS, C), BF16),
            jax.ShapeDtypeStruct((64, C), F32),
            jax.ShapeDtypeStruct((16, 512), F32),
            jax.ShapeDtypeStruct((16, C), F32),
        ),
        in_specs=[SMEM] + [pl.BlockSpec(memory_space=pl.ANY)] * 2 + [VMEM] * 8,
        out_specs=[VMEM] * 5,
        scratch_shapes=[
            v(CAP, ROWS, C), v(CAP, ROWS, C), v(16, 512), v(16, C), v(128, 128, dtype=F32),
            v(9, ROWS, C), v(9, ROWS, C), v(3, ROWS, C), v(3, ROWS, 128), v(3, ROWS, 128), v(3, ROWS, 128), v(6, ROWS, C), v(6, ROWS, C),
            v(4, 16, 512), v(4, 16, C), v(2, 3, 4, 4, 16, 512), v(2, 3, 4, 4, 16, C),
            v(XC, 3, RP, 128, dtype=F32), v(XC, 3, RP, 128, dtype=F32),
            v(49, 3, 8, 128, dtype=F32), v(49, 3, 8, 128, dtype=F32),
            v(NC, 3, ROWS, 128, dtype=F32), v(NC, ROWS, C),
            v(TOK, 512), v(512, TOK), v(TOK, C), v(C, TOK), v(TOK, C, dtype=F32), v(TOK, 128, dtype=F32), v(TOK, C, dtype=F32),
            v(TOK, 256), v(TOK, 256), v(TOK, 256), v(TOK, 256), v(512, 256), v(C, 256), v(256, C),
            v(8, 8, C, dtype=F32), v(NC, ROWS, C),
            v(3, 4, 4, 16, 512), v(3, 4, 4, 16, C), v(2, 3, ROWS, C), v(2, 3, ROWS, C),
            v(3, 4, 4, 16, 512), v(3, 4, 4, 16, C), v(3, 4, 4, 16, 512), v(3, 4, 4, 16, C),
            v(3, 3, 4, 16, 512), v(3, 3, 4, 16, C), v(3, 4, 16, 512), v(3, 4, 16, C), v(3, 3, 16, 512), v(3, 3, 16, C),
            v(4, 16, 512, dtype=F32), v(4, 16, C, dtype=F32), v(3, 16, 512, dtype=F32), v(3, 16, C, dtype=F32),
            v(49, 3, 8, 128, dtype=F32), v(64, C, dtype=F32), v(2, 2, 16, C, dtype=F32), v(2, 16, C, dtype=F32),
            v(4, 2, 16, C, dtype=F32), v(18, 16, C, dtype=F32), v(2, 2, 16, C, dtype=F32),
            v(NC, ROWS, C), v(6, ROWS, C), v(6, ROWS, C),
            pltpu.SemaphoreType.DMA((131,)), pltpu.SemaphoreType.DMA((131,)), pltpu.SemaphoreType.DMA((2,)),
        ],
        compiler_params=pltpu.CompilerParams(collective_id=0, has_side_effects=True, vmem_limit_bytes=60 * 2**20),
        name="block_back",
    )(*args)


def local(features, grad_out, widths, dw_kernel, dw_bias, ln_gain, ln_bias,
          w_in, in_bias, w_out, out_bias, layer_scale):
    feat, cot = jnp.transpose(features, (1, 0, 2)), jnp.transpose(grad_out, (1, 0, 2))
    place = lax.axis_index("strip").reshape(1)
    dimg, rmate, total, o1, o2 = fused(widths, feat, cot, w_in.T, in_bias, w_out, dw_kernel,
                                       dw_bias, ln_gain, ln_bias, layer_scale)
    outs = finish(widths, place, dimg, rmate, total, o1, o2, out_bias, layer_scale)
    return (jnp.transpose(outs[0], (1, 0, 2)),) + tuple(outs[1:5]) + (outs[5].T,) + tuple(outs[6:])


def solution(mesh):
    wide = P(None, "strip", None)
    return jax.shard_map(
        local, mesh=mesh,
        in_specs=(wide, wide, P(), P(), P(), P(), P(), P(None, "strip"), P("strip"), P("strip", None), P(), P()),
        out_specs=(wide, P(), P(), P(), P(), P(None, "strip"), P("strip"), P("strip", None), P(), P()),
        check_vma=False)
```
